256 devices in a mesh: seq: 8 (over y, core), mp: 32 (over z, x).
Axes of the slice: x: 4, y: 4, z: 8, core: 2. Of those that a mesh axis runs over, the one named last changes fastest.
Arguments:
- tokens: bfloat16 [4096, 8192], P('seq', 'mp')
- norm_gain: float32 [8192], replicated, may hold values from 0.1 to 1.9
- query_weight: bfloat16 [8192, 8192], P(None, 'mp')
- pair_weight: bfloat16 [8192, 2048], P(None, 'mp')
- ancestors: int32 [32, 5], replicated, may hold values from -1 to 30, as said below
- out_weight: bfloat16 [8192, 8192], P('mp'), may hold values from -0.125 to 0.125
Outputs:
- mixed: bfloat16 [4096, 8192], P('seq', 'mp')
The draws below stay inside these ranges and needn't reach their ends.
Inputs may be any that keep to these rules, and one draw needn't show every extreme that they name: `ancestors`: one tree of 32 blocks starts with 4 prompt blocks; a prompt block lists the earlier prompt blocks. Every later block is a response block: it lists a leading run of 1 to 4 prompt blocks in its first entries and, in its last entry, either -1 or its parent, an earlier response block, whose leading run of prompt blocks it shares. The first response block lists all prompt blocks and no parent; the last block's parent is the block before it. Unused entries are -1; a block never lists itself.
All inputs are finite; a program needn't handle non-finite values.
Results may differ from the reference program's by a relative error of at most 0.0095.
Values may be sent and summed in bfloat16 or wider, within the bound.
A program may use at most 128 MiB of HBM per device.

```python
import math
import jax
import jax.numpy as jnp
from jax import lax

D = 8192
HQ = 64
KVH = 8
HD = 128
BLK = 128
PROMPT_BLK = 4
TOKENS = 4096
NB = 32
MAXA = 5


def pair_weight_base(key):
    return jax.random.normal(jax.random.fold_in(key, 21), (D, 2 * KVH * HD), jnp.float32) / math.sqrt(D)


def draw_pair_weight(key, part):
    return pair_weight_base(key).astype(jnp.bfloat16)


def draw_query_weight(key, part):
    base_weight = jax.random.normal(jax.random.fold_in(key, 22), (D, HQ * HD), jnp.float32) / math.sqrt(D)
    return base_weight.astype(jnp.bfloat16)


def draw_tokens(key, part):
    row_scale = jnp.exp(jax.random.uniform(jax.random.fold_in(key, 1), (TOKENS, 1), jnp.float32, 0.0, math.log(10.0)))
    column_scale = jnp.exp(math.log(10.0) * jnp.arange(D, dtype=jnp.float32) / D + jax.random.uniform(jax.random.fold_in(key, 2), (D,), jnp.float32, -0.7, 0.7))
    base_value = jax.random.normal(jax.random.fold_in(key, 3), (TOKENS, D), jnp.float32)
    return (base_value * row_scale * column_scale[None, :]).astype(jnp.bfloat16)


def draw_ancestors(key, part):
    key = jax.random.fold_in(key, 31)
    prompt_raw = jax.random.randint(jax.random.fold_in(key, 1), (NB,), 1, PROMPT_BLK + 1, dtype=jnp.int32)
    parent_raw = jax.random.randint(jax.random.fold_in(key, 2), (NB,), 0, NB, dtype=jnp.int32)

    def place_block(index, carry):
        prompt_count, parent_ids = carry
        earlier = jnp.maximum(index - PROMPT_BLK, 0)
        picked = parent_raw[index] % (earlier + 1)
        parent = jnp.where(picked == 0, -1, PROMPT_BLK + picked - 1)
        parent = jnp.where(index == NB - 1, NB - 2, parent)
        parent = jnp.where(index >= PROMPT_BLK, parent, -1).astype(jnp.int32)
        count = jnp.where(parent >= 0, prompt_count[jnp.maximum(parent, 0)], prompt_raw[index])
        count = jnp.where(index <= PROMPT_BLK, PROMPT_BLK, count).astype(jnp.int32)
        return (prompt_count.at[index].set(count), parent_ids.at[index].set(parent))
    start_carry = (jnp.zeros((NB,), jnp.int32), jnp.full((NB,), -1, jnp.int32))
    prompt_count, parent_ids = lax.fori_loop(0, NB, place_block, start_carry)
    block_ids = jnp.arange(NB, dtype=jnp.int32)
    slot_ids = jnp.arange(MAXA, dtype=jnp.int32)
    is_response = block_ids >= PROMPT_BLK
    seen = jnp.where(is_response, prompt_count, block_ids)
    prompt_part = jnp.where(slot_ids[None, :] < seen[:, None], slot_ids[None, :], -1)
    last_entry = jnp.where(is_response, parent_ids, -1)
    return jnp.where(slot_ids[None, :] < PROMPT_BLK, prompt_part, last_entry[:, None]).astype(jnp.int32)


def raised(values, stream_key, source, target, shards_of, factor):
    def block_of(position):
        return (jnp.arange(values.shape[position]) // (values.shape[position] // shards_of)).reshape((-1,) + (1,) * (values.ndim - 1 - position))

    near = jax.random.permutation(stream_key, shards_of)[block_of(target)]
    far = (block_of(target) + shards_of // 2) % shards_of
    return jnp.where((block_of(source) == near) | (block_of(source) == far), factor * values, values)


def block_scale(own_key, dims, shards, smallest, high):
    gain, own = 1.0, jax.random.fold_in(own_key, 6)
    for position, shards_of in shards:
        draws = jnp.exp(jax.random.uniform(jax.random.fold_in(own, position), (shards_of,), jnp.float32, smallest / len(shards), high / len(shards)))
        gain = gain * jnp.repeat(draws, dims[position] // shards_of).reshape([-1 if axis == position else 1 for axis in range(len(dims))])
    return gain


def bell_draw_with(own_key, dims, deviation, bound, cuts, heavy, kind=jnp.bfloat16):
    drawn = deviation * jax.random.normal(own_key, dims, jnp.float32)
    if cuts:
        drawn = drawn * block_scale(own_key, dims, cuts, -0.22, 0.18)
    return jnp.clip(raised(drawn, jax.random.fold_in(own_key, 3), *heavy), -bound, bound).astype(kind)


def setup_inputs(seed: int = 0) -> dict:
    splits = jax.random.split(jax.random.key(seed), 7)
    tokens = draw_tokens(jax.random.fold_in(splits[6], 71), 0)
    norm_gain = jnp.clip(1.0 + 0.18 * jax.random.normal(splits[1], (D,), jnp.float32), 0.1, 1.9)
    query_weight = draw_query_weight(jax.random.fold_in(splits[6], 71), 0)
    pair_weight = draw_pair_weight(jax.random.fold_in(splits[6], 71), 0)
    ancestors = draw_ancestors(jax.random.fold_in(splits[6], 71), 0)
    out_weight = bell_draw_with(splits[5], (HQ * HD, D), (HQ * HD) ** -0.5, 0.125, ((0, 32),), (0, 1, 32, 2.75))
    return dict(tokens=tokens, norm_gain=norm_gain, query_weight=query_weight, pair_weight=pair_weight, ancestors=ancestors, out_weight=out_weight)


def reference(tokens, norm_gain, query_weight, pair_weight, ancestors, out_weight):
    tok_float = tokens.astype(jnp.float32)
    mean_square = lax.optimization_barrier(jnp.mean(tok_float * tok_float, axis=1, keepdims=True))
    normed = (tok_float * lax.rsqrt(mean_square + 1e-05) * norm_gain).astype(jnp.bfloat16)
    queries = jnp.dot(normed, query_weight, preferred_element_type=jnp.float32).astype(jnp.bfloat16)
    kv_pairs = jnp.dot(normed, pair_weight, preferred_element_type=jnp.float32).astype(jnp.bfloat16)
    queries = lax.optimization_barrier(queries)
    kv_pairs = lax.optimization_barrier(kv_pairs)
    num_blocks = TOKENS // BLK
    kv_group = HQ // KVH
    key_table = kv_pairs[:, :KVH * HD].astype(jnp.float32).reshape(TOKENS, KVH, HD)
    value_table = kv_pairs[:, KVH * HD:].astype(jnp.float32).reshape(TOKENS, KVH, HD)
    block_ids = jnp.arange(num_blocks, dtype=jnp.int32)
    list_table = jnp.any(ancestors[:, :, None] == block_ids[None, None, :], axis=1)
    key_block = jnp.arange(TOKENS, dtype=jnp.int32) // BLK
    key_offset = jnp.arange(TOKENS, dtype=jnp.int32) % BLK
    query_offset = jnp.arange(BLK, dtype=jnp.int32)
    query_blocks = queries.astype(jnp.float32).reshape(num_blocks, BLK, KVH, kv_group, HD)

    def one_block(block_item):
        query_block, block_list, block_index = block_item
        visible = block_list[key_block][None, :] | (key_block == block_index)[None, :] & (key_offset[None, :] <= query_offset[:, None])
        scores = jnp.einsum('tgrd,ugd->grtu', query_block, key_table, precision=lax.Precision.HIGHEST) * HD ** (-0.5)
        masked_scores = jnp.where(visible[None, None], scores, -1e+30)
        row_max = lax.optimization_barrier(jnp.max(masked_scores, axis=3, keepdims=True))
        weights = jnp.where(visible[None, None], jnp.exp(masked_scores - row_max), 0.0)
        weight_sum = lax.optimization_barrier(jnp.sum(weights, axis=3))
        rounded = lax.optimization_barrier(weights.astype(jnp.bfloat16)).astype(jnp.float32)
        weighted_sum = jnp.einsum('grtu,ugd->tgrd', rounded, value_table, precision=lax.Precision.HIGHEST)
        result = weighted_sum / jnp.transpose(weight_sum, (2, 0, 1))[..., None]
        return result.astype(jnp.bfloat16).reshape(BLK, HQ * HD)
    attended = lax.map(one_block, (query_blocks, list_table, block_ids)).reshape(TOKENS, HQ * HD)
    return jnp.dot(attended, out_weight, preferred_element_type=jnp.float32).astype(jnp.bfloat16)
```

```python
import functools

import jax
import jax.numpy as jnp
from jax import lax
from jax.experimental import pallas as pl
from jax.experimental.pallas import tpu as pltpu
from jax.sharding import PartitionSpec as P

MESH = pl.DeviceIdType.MESH
HD = 128
BLK = 128
NX, NY, NZ = 4, 4, 8
FEATURES = 8192
EPS = 1e-05
NEG = -1e30
F32 = jnp.float32
BF16 = jnp.bfloat16


def nt_dot(a, b):
    return lax.dot_general(a, b, (((1,), (1,)), ((), ())), preferred_element_type=F32)


def kernel(
    anc, gain, tok, wq, pwt, wo, out,
    xg, xn, rcol, ssx, ssz, wb, wob, kvs, kvr, kvown, kvtab, qs, qr, qown, qb, attb, rsend, rrecv,
    local_sem, x_s, x_r, ssx_s, ssx_r, ssz_s, ssz_r,
    w_s, w_r, p_s, p_r, wy_s, wy_r, wc_s, wc_r,
    o_s, o_r, oy_s, oy_r, oc_s, oc_r,
    kv_s, kv_r, ka_s, ka_r, ky_s, ky_r, kc_s, kc_r, q_s, q_r, at_s, at_r, rs_s, rs_r,
):
    s = lax.axis_index("seq")
    m = lax.axis_index("mp")
    y, c = s // 2, s % 2
    z, x = m // NX, m % NX

    def at_x(d):
        return (s, z * NX + (x + d) % NX)

    def at_z(k):
        return (s, ((z + k + NZ) % NZ) * NX + x)

    def at_y(e):
        return (((y + e) % NY) * 2 + c, m)

    sibling = (y * 2 + 1 - c, m)

    def lane_strip(e):
        return ((y + e) % NY) * 2 + c

    def far_strip(e):
        return ((y + e) % NY) * 2 + 1 - c

    def remote(src, dst, ss, rs, dev):
        return pltpu.make_async_remote_copy(
            src_ref=src, dst_ref=dst, send_sem=ss, recv_sem=rs, device_id=dev, device_id_type=MESH
        )

    pair_q = (m // 16) * 2 + m % 2
    pair_z = (m // 2) % NZ

    barrier = pltpu.get_barrier_semaphore()
    peers = [at_x(d) for d in (1, 2, 3)] + [at_z(k) for k in range(1, NZ)] + [at_y(e) for e in (1, 2, 3)] + [sibling]
    for dev in peers:
        pl.semaphore_signal(barrier, inc=1, device_id=dev, device_id_type=MESH)
    for source in (2 * z, 2 * z + 1, 16 + 2 * z, 17 + 2 * z):

        @pl.when(source != m)
        def _():
            pl.semaphore_signal(barrier, inc=1, device_id=(s, source), device_id_type=MESH)

    own_x = pltpu.make_async_copy(tok, xg.at[z], local_sem.at[0])
    own_x.start()
    own_w = pltpu.make_async_copy(wq.at[:, x], wb.at[0], local_sem.at[1])
    own_w.start()
    pl.semaphore_wait(barrier, len(peers) + jnp.where(pair_z == z, 3, 4))

    def rows(b):
        return pl.ds(b * BLK, BLK)

    def x_copy(way, hop, b):
        step = 1 if way == 0 else -1
        shard = (z - step * hop + NZ) % NZ
        src = tok.at[rows(b)] if hop == 0 else xg.at[shard, rows(b)]
        return remote(src, xg.at[shard, rows(b)], x_s.at[way, hop, b], x_r.at[way, hop, b], at_z(step))

    def x_arrival(way, hop, b):
        step = 1 if way == 0 else -1
        shard = (z - step * (hop + 1) + NZ) % NZ
        ref = xg.at[shard, rows(b)]
        return remote(ref, ref, x_s.at[way, hop, b], x_r.at[way, hop, b], at_z(step))

    def x_used(way, hop, b):
        return hop < 3 or (b < 2) == (way == 0)

    for b in range(4):
        for way in range(2):
            x_copy(way, 0, b).start()

    def w_copy(i, d):
        strip = lane_strip(2 * i)
        return remote(wq.at[strip, (x + d) % NX], wb.at[4 - d, strip], w_s.at[i, d - 1], w_r.at[i, 3 - d], at_x(d))

    def p_copy(i, x2):
        strip = lane_strip(2 * i)
        src = pwt.at[:, pl.ds(pl.multiple_of((strip * NX + x2) * 256, 256), 256)]
        dst = wb.at[4, strip, pl.ds(pl.multiple_of(pair_q * 64, 64), 64), :]
        return remote(src, dst, p_s.at[i, x2], p_r.at[i, pair_q], (s, pair_z * NX + x2)), src, dst

    def p_self(x2):
        return jnp.logical_and(pair_z == z, x == x2)

    def p_start(i):
        for x2 in range(NX):
            cp, src, dst = p_copy(i, x2)

            @pl.when(p_self(x2))
            def _():
                pltpu.make_async_copy(src, dst, p_r.at[i, pair_q]).start()

            @pl.when(jnp.logical_not(p_self(x2)))
            def _():
                cp.start()

    for i in range(2):
        for d in (1, 3, 2):
            w_copy(i, d).start()
        p_start(i)

    own_x.wait()
    row_id = lax.broadcasted_iota(jnp.int32, (8, BLK), 0)
    part = jnp.zeros((8, BLK), F32)
    for b in range(4):
        xf = xg[z, b * BLK : (b + 1) * BLK, :].astype(F32)
        sums = jnp.broadcast_to(jnp.sum(xf * xf, axis=1, keepdims=True), (BLK, BLK)).T
        part = jnp.where(row_id == b, sums[:8], part)
    ssx[0] = part

    def ssx_copy(d):
        return remote(ssx.at[0], ssx.at[4 - d], ssx_s.at[d - 1], ssx_r.at[3 - d], at_x(d))

    def ssz_copy(k):
        return remote(ssz.at[0], ssz.at[NZ - k], ssz_s.at[k - 1], ssz_r.at[NZ - 1 - k], at_z(k))

    for d in (1, 3, 2):
        ssx_copy(d).start()

    def x_forward(hop):
        for b in range(4):
            for way in range(2):
                if x_used(way, hop, b):
                    x_arrival(way, hop, b).wait_recv()
                    if hop < 3 and x_used(way, hop + 1, b):
                        x_copy(way, hop + 1, b).start()

    x_forward(0)
    for d in (1, 2, 3):
        ssx_copy(d).wait_recv()
    ssz[0] = ssx[0] + ssx[1] + ssx[2] + ssx[3]
    for k in (1, 7, 2, 6, 3, 5, 4):
        ssz_copy(k).start()

    def wy_copy(e):
        src = wb.at[pl.ds(1, 4), s]
        return remote(src, src, wy_s.at[e // 2], wy_r.at[(3 - e) // 2], at_y(e))

    def wy_arrival(e):
        ref = wb.at[pl.ds(1, 4), lane_strip(e)]
        return remote(ref, ref, wy_s.at[e // 2], wy_r.at[e // 2], at_y(e))

    def wc_copy(e):
        src = wb.at[pl.ds(1, 4), lane_strip(e)]
        return remote(src, src, wc_s.at[e], wc_r.at[e], sibling)

    def wc_arrival(e):
        ref = wb.at[pl.ds(1, 4), far_strip(e)]
        return remote(ref, ref, wc_s.at[e], wc_r.at[e], sibling)

    def w_arrive(i):
        strip = lane_strip(2 * i)
        for d in (1, 2, 3):
            ref = wb.at[d, strip]
            remote(ref, ref, w_s.at[i, d - 1], w_r.at[i, d - 1], at_x(d)).wait_recv()
        for q in range(4):
            ref = wb.at[4, strip, pl.ds(q * 64, 64), :]
            remote(ref, ref, p_s.at[i, q], p_r.at[i, q], sibling).wait_recv()

    w_arrive(0)
    wy_copy(1).start()
    wy_copy(3).start()
    wc_copy(0).start()
    x_forward(1)

    for k in range(1, NZ):
        ssz_copy(k).wait_recv()
    total = ssz[0]
    for k in range(1, NZ):
        total = total + ssz[k]
    scale = lax.rsqrt(total * (1.0 / FEATURES) + EPS)
    for b in range(4):
        rcol[b] = jnp.broadcast_to(scale[b : b + 1, :], (BLK, BLK)).T

    def normalise(shard):
        g = gain[pl.ds(shard * NX + x, 1), :]

        def one(b, carry):
            at = pl.ds(pl.multiple_of(b * BLK, BLK), BLK)
            r = rcol[b]
            v = xg[shard, at, :].astype(F32) * jnp.concatenate([r, r], axis=1) * g
            xn[at, pl.ds(pl.multiple_of(shard * 256, 256), 256)] = v.astype(BF16)
            return carry

        lax.fori_loop(0, 4, one, 0)

    normalise(z)
    normalise((z + 1) % NZ)
    normalise((z + 7) % NZ)
    w_arrive(1)
    wc_copy(2).start()

    def wo_block(strip, x2):
        return wo.at[:, pl.ds(pl.multiple_of((strip * NX + x2) * 256, 256), 256)]

    own_wo = [pltpu.make_async_copy(wo_block(k, x), wob.at[0, k], local_sem.at[2 + k]) for k in range(NZ)]
    for cp in own_wo:
        cp.start()

    def o_copy(i, d):
        strip = lane_strip(2 * i)
        return remote(wo_block(strip, (x + d) % NX), wob.at[4 - d, strip], o_s.at[i, d - 1], o_r.at[i, 3 - d], at_x(d))

    def oy_copy(e):
        src = wob.at[pl.ds(1, 3), s]
        return remote(src, src, oy_s.at[e // 2], oy_r.at[(3 - e) // 2], at_y(e))

    def oy_arrival(e):
        ref = wob.at[pl.ds(1, 3), lane_strip(e)]
        return remote(ref, ref, oy_s.at[e // 2], oy_r.at[e // 2], at_y(e))

    def oc_copy(e):
        src = wob.at[pl.ds(1, 3), lane_strip(e)]
        return remote(src, src, oc_s.at[e], oc_r.at[e], sibling)

    def oc_arrival(e):
        ref = wob.at[pl.ds(1, 3), far_strip(e)]
        return remote(ref, ref, oc_s.at[e], oc_r.at[e], sibling)

    def o_arrive(i):
        strip = lane_strip(2 * i)
        for d in (1, 2, 3):
            ref = wob.at[d, strip]
            remote(ref, ref, o_s.at[i, d - 1], o_r.at[i, d - 1], at_x(d)).wait_recv()

    for i in range(2):
        for d in (1, 3, 2):
            o_copy(i, d).start()

    x_forward(2)
    normalise((z + 2) % NZ)
    normalise((z + 6) % NZ)
    for e in (1, 3):
        wy_arrival(e).wait_recv()
        wc_copy(e).start()
    normalise((z + 3) % NZ)
    normalise((z + 5) % NZ)
    x_forward(3)
    normalise((z + 4) % NZ)
    for e in range(4):
        wc_arrival(e).wait_recv()
    own_w.wait()

    acc = nt_dot(xn[:, :256], wb[4, 0])
    for k in range(1, NZ):
        acc = acc + nt_dot(xn[:, k * 256 : (k + 1) * 256], wb[4, k])
    kvown[...] = acc.reshape(4, BLK, 256)
    kvs[...] = acc.astype(BF16).reshape(4, BLK, 256)

    def kv_copy(d):
        return remote(kvs.at[(x + d) % NX], kvr.at[3 - d], kv_s.at[d - 1], kv_r.at[3 - d], at_x(d))

    for d in (1, 3, 2):
        kv_copy(d).start()

    def q_copy(xa, d):
        return remote(qs.at[xa, (x + d) % NX], qr.at[3 - d, xa], q_s.at[xa, d - 1], q_r.at[xa, 3 - d], at_x(d))

    def q_part(d, carry):
        xa = (x + d) % NX
        a = jnp.dot(xn[...], wb[d].reshape(2048, 256), preferred_element_type=F32).reshape(4, BLK, 256)
        qs[xa] = a.astype(BF16)
        qown[xa] = a
        for e in (1, 3, 2):
            q_copy(xa, e).start()
        return carry

    lax.fori_loop(0, 4, q_part, 0)

    block = s * NX + x
    for d in (1, 2, 3):
        kv_copy(d).wait_recv()
    mine = kvown[x] + kvr[0].astype(F32) + kvr[1].astype(F32) + kvr[2].astype(F32)
    kvtab[block] = mine.astype(BF16)

    def ka_copy(d):
        return remote(kvtab.at[block], kvtab.at[block], ka_s.at[d - 1], ka_r.at[3 - d], at_x(d))

    def ka_arrival(d):
        ref = kvtab.at[s * NX + (x + d) % NX]
        return remote(ref, ref, ka_s.at[d - 1], ka_r.at[d - 1], at_x(d))

    for d in (1, 3, 2):
        ka_copy(d).start()
    o_arrive(0)
    oy_copy(1).start()
    oy_copy(3).start()
    oc_copy(0).start()

    def group(strip):
        return kvtab.at[pl.ds(strip * NX, NX)]

    def ky_copy(e):
        return remote(group(s), group(s), ky_s.at[e - 1], ky_r.at[3 - e], at_y(e))

    def ky_arrival(e):
        ref = group(lane_strip(e))
        return remote(ref, ref, ky_s.at[e - 1], ky_r.at[e - 1], at_y(e))

    def kc_copy(e):
        ref = group(lane_strip(e))
        return remote(ref, ref, kc_s.at[e], kc_r.at[e], sibling)

    def kc_arrival(e):
        ref = group(far_strip(e))
        return remote(ref, ref, kc_s.at[e], kc_r.at[e], sibling)

    for d in (1, 3, 2):
        ka_arrival(d).wait_recv()
    for e in (1, 3, 2):
        ky_copy(e).start()
    kc_copy(0).start()

    o_arrive(1)
    oc_copy(2).start()

    for xa in range(NX):
        for d in (1, 2, 3):
            q_copy(xa, d).wait_recv()
        v = qown[xa, x] + qr[0, xa].astype(F32) + qr[1, xa].astype(F32) + qr[2, xa].astype(F32)
        qb[xa] = v.astype(BF16)

    for e in (1, 3):
        oy_arrival(e).wait_recv()
        oc_copy(e).start()
    for e in (1, 3, 2):
        ky_arrival(e).wait_recv()
        kc_copy(e).start()
    for e in range(4):
        kc_arrival(e).wait_recv()

    listed = [anc[block, j] for j in range(5)]
    tables = [kvtab[jnp.maximum(i, 0)] for i in listed] + [kvtab[block]]
    causal = lax.broadcasted_iota(jnp.int32, (BLK, BLK), 0) >= lax.broadcasted_iota(jnp.int32, (BLK, BLK), 1)
    causal = jnp.concatenate([causal, causal], axis=0)
    for xa in range(NX):
        q2 = jnp.concatenate([qb[xa, :, :HD], qb[xa, :, HD:]], axis=0)
        masks, scores = [], []
        for j in range(6):
            sc = nt_dot(q2, tables[j][:, :HD]) * HD**-0.5
            ok = causal if j == 5 else jnp.broadcast_to(listed[j], (2 * BLK, BLK)) >= 0
            masks.append(ok)
            scores.append(jnp.where(ok, sc, NEG))
        top = functools.reduce(jnp.maximum, scores)
        top = jnp.max(top, axis=1, keepdims=True)
        weights = [jnp.where(ok, jnp.exp(sc - top), 0.0) for ok, sc in zip(masks, scores)]
        total = jnp.sum(functools.reduce(jnp.add, weights), axis=1, keepdims=True)
        got = jnp.zeros((2 * BLK, HD), F32)
        for j in range(6):
            got = got + jnp.dot(weights[j].astype(BF16), tables[j][:, HD:], preferred_element_type=F32)
        got = (got / total).astype(BF16)
        attb[x, xa] = jnp.concatenate([got[:BLK], got[BLK:]], axis=1)

    def at_copy(d):
        return remote(attb.at[x], attb.at[x], at_s.at[d - 1], at_r.at[3 - d], at_x(d))

    def at_arrival(d):
        ref = attb.at[(x + d) % NX]
        return remote(ref, ref, at_s.at[d - 1], at_r.at[d - 1], at_x(d))

    for d in (1, 3, 2):
        at_copy(d).start()
    for cp in own_wo:
        cp.wait()
    for e in range(4):
        oc_arrival(e).wait_recv()

    order = (0, 1, 3, 2)

    def term(d, shard):
        b = (x + d) % NX
        a = jnp.dot(attb[b, x], wob[0, shard], preferred_element_type=F32)
        for e in range(1, NX):
            a = a + jnp.dot(attb[b, (x + e) % NX], wob[e, shard], preferred_element_type=F32)
        return a

    def r_copy(way, k, d):
        step = 1 if way == 0 else -1
        return remote(
            rsend.at[way, k - 1, d], rrecv.at[way, k - 1, d], rs_s.at[way, k - 1, d], rs_r.at[way, k - 1, d], at_z(step)
        )

    def long_way(i):
        return i % 2

    def r_step(way, k, d, longest):
        step = 1 if way == 0 else -1
        v = term(d, (z + step * k + NZ) % NZ)
        if k < longest:
            r_copy(way, k + 1, d).wait_recv()
            v = v + rrecv[way, k, d].astype(F32)
        rsend[way, k - 1, d] = v.astype(BF16)
        r_copy(way, k, d).start()

    sent = []
    for t in range(8):
        for i, d in enumerate(order):
            stage = t - i
            if stage < 0 or stage > 4:
                continue
            far = long_way(i)
            if stage == 0 and d > 0:
                at_arrival(d).wait_recv()
            if stage < 4:
                r_step(far, 4 - stage, d, 4)
                sent.append((far, 4 - stage, d))
            if stage < 3:
                r_step(1 - far, 3 - stage, d, 3)
                sent.append((1 - far, 3 - stage, d))
            if stage == 4:
                v = term(d, z)
                for way in range(2):
                    r_copy(way, 1, d).wait_recv()
                    v = v + rrecv[way, 0, d].astype(F32)
                out[pl.ds(pl.multiple_of(((x + d) % NX) * BLK, BLK), BLK), :] = v.astype(BF16)

    for way, k, d in sent:
        r_copy(way, k, d).wait_send()
    for b in range(4):
        for way in range(2):
            for hop in range(4):
                if x_used(way, hop, b):
                    x_copy(way, hop, b).wait_send()
    for i in range(2):
        for d in (1, 2, 3):
            w_copy(i, d).wait_send()
            o_copy(i, d).wait_send()
        for x2 in range(NX):
            cp = p_copy(i, x2)[0]

            @pl.when(jnp.logical_not(p_self(x2)))
            def _():
                cp.wait_send()

    for d in (1, 2, 3):
        ssx_copy(d).wait_send()
        kv_copy(d).wait_send()
        ka_copy(d).wait_send()
        at_copy(d).wait_send()
        ky_copy(d).wait_send()
        for xa in range(NX):
            q_copy(xa, d).wait_send()
    for k in range(1, NZ):
        ssz_copy(k).wait_send()
    for e in (1, 3):
        wy_copy(e).wait_send()
        oy_copy(e).wait_send()
    for e in range(4):
        wc_copy(e).wait_send()
        oc_copy(e).wait_send()
        kc_copy(e).wait_send()


def local(tokens, norm_gain, query_weight, pair_weight, ancestors, out_weight):
    dma = pltpu.SemaphoreType.DMA
    any_ = pl.BlockSpec(memory_space=pl.ANY)
    vmem = pl.BlockSpec(memory_space=pltpu.VMEM)
    vm = pltpu.VMEM
    return pl.pallas_call(
        kernel,
        out_shape=jax.ShapeDtypeStruct((512, 256), BF16),
        in_specs=[pl.BlockSpec(memory_space=pltpu.SMEM), vmem, any_, any_, any_, any_],
        out_specs=vmem,
        scratch_shapes=[
            vm((8, 512, 256), BF16),
            vm((512, 2048), BF16),
            vm((4, 128, 128), F32),
            vm((4, 8, 128), F32),
            vm((8, 8, 128), F32),
            vm((5, 8, 256, 256), BF16),
            vm((4, 8, 256, 256), BF16),
            vm((4, 128, 256), BF16),
            vm((3, 128, 256), BF16),
            vm((4, 128, 256), F32),
            vm((32, 128, 256), BF16),
            vm((4, 4, 128, 256), BF16),
            vm((3, 4, 128, 256), BF16),
            vm((4, 4, 128, 256), F32),
            vm((4, 128, 256), BF16),
            vm((4, 4, 128, 256), BF16),
            vm((2, 4, 4, 128, 256), BF16),
            vm((2, 4, 4, 128, 256), BF16),
            dma((10,)),
            dma((2, 4, 4)), dma((2, 4, 4)), dma((3,)), dma((3,)), dma((7,)), dma((7,)),
            dma((2, 3)), dma((2, 3)), dma((2, 4)), dma((2, 4)), dma((2,)), dma((2,)), dma((4,)), dma((4,)),
            dma((2, 3)), dma((2, 3)), dma((2,)), dma((2,)), dma((4,)), dma((4,)),
            dma((3,)), dma((3,)), dma((3,)), dma((3,)), dma((3,)), dma((3,)), dma((4,)), dma((4,)),
            dma((4, 3)), dma((4, 3)), dma((3,)), dma((3,)), dma((2, 4, 4)), dma((2, 4, 4)),
        ],
        compiler_params=pltpu.CompilerParams(collective_id=0, has_side_effects=True, vmem_limit_bytes=50 << 20),
        cost_estimate=pl.CostEstimate(flops=6 * 10**9, bytes_accessed=10 << 20, transcendentals=10**6),
        name="tree_attention",
    )(
        ancestors,
        norm_gain.reshape(32, 256),
        tokens,
        query_weight.reshape(8, 4, 256, 256),
        pair_weight.T,
        out_weight,
    )


def solution(mesh):
    return jax.shard_map(
        local,
        mesh=mesh,
        in_specs=(P("seq", "mp"), P(), P(None, "mp"), P(None, "mp"), P(), P("mp", None)),
        out_specs=P("seq", "mp"),
        check_vma=False,
    )
```

```python
import functools

import jax
import jax.numpy as jnp
from jax import lax
from jax.experimental import pallas as pl
from jax.experimental.pallas import tpu as pltpu
from jax.sharding import PartitionSpec as P

MESH = pl.DeviceIdType.MESH
HD = 128
BLK = 128
NX, NY, NZ = 4, 4, 8
FEATURES = 8192
EPS = 1e-05
NEG = -1e30
F32 = jnp.float32
BF16 = jnp.bfloat16


def nt_dot(a, b):
    return lax.dot_general(a, b, (((1,), (1,)), ((), ())), preferred_element_type=F32)


def kernel(
    anc, gain, tok, wq, pwt, wo, out,
    xg, xn, rcol, ssx, ssz, wb, wob, kvs, kvr, kvown, kvtab, qs, qr, qown, qb, attb, rsend, rrecv,
    local_sem, x_s, x_r, ssx_s, ssx_r, ssz_s, ssz_r,
    w_s, w_r, p_s, p_r, wy_s, wy_r, wf_s, wf_r, wc_s, wc_r,
    o_s, o_r, oy_s, oy_r, oc_s, oc_r,
    kv_s, kv_r, ka_s, ka_r, ky_s, ky_r, kc_s, kc_r, q_s, q_r, at_s, at_r, af_s, af_r, rs_s, rs_r,
):
    s = lax.axis_index("seq")
    m = lax.axis_index("mp")
    y, c = s // 2, s % 2
    z, x = m // NX, m % NX

    def at_x(d):
        return (s, z * NX + (x + d) % NX)

    def at_z(k):
        return (s, ((z + k + NZ) % NZ) * NX + x)

    def at_y(e):
        return (((y + e) % NY) * 2 + c, m)

    sibling = (y * 2 + 1 - c, m)

    def lane_strip(e):
        return ((y + e) % NY) * 2 + c

    def far_strip(e):
        return ((y + e) % NY) * 2 + 1 - c

    def remote(src, dst, ss, rs, dev):
        return pltpu.make_async_remote_copy(
            src_ref=src, dst_ref=dst, send_sem=ss, recv_sem=rs, device_id=dev, device_id_type=MESH
        )

    pair_q = (m // 16) * 2 + m % 2
    pair_z = (m // 2) % NZ

    barrier = pltpu.get_barrier_semaphore()
    peers = [at_x(d) for d in (1, 2, 3)] + [at_z(k) for k in range(1, NZ)] + [at_y(e) for e in (1, 2, 3)] + [sibling]
    for dev in peers:
        pl.semaphore_signal(barrier, inc=1, device_id=dev, device_id_type=MESH)
    for source in (2 * z, 2 * z + 1, 16 + 2 * z, 17 + 2 * z):

        @pl.when(source != m)
        def _():
            pl.semaphore_signal(barrier, inc=1, device_id=(s, source), device_id_type=MESH)

    own_x = pltpu.make_async_copy(tok, xg.at[z], local_sem.at[0])
    own_x.start()
    own_w = pltpu.make_async_copy(wq.at[:, x], wb.at[0], local_sem.at[1])
    own_w.start()
    pl.semaphore_wait(barrier, len(peers) + jnp.where(pair_z == z, 3, 4))

    def rows(b):
        return pl.ds(b * BLK, BLK)

    def x_copy(way, hop, b):
        step = 1 if way == 0 else -1
        shard = (z - step * hop + NZ) % NZ
        src = tok.at[rows(b)] if hop == 0 else xg.at[shard, rows(b)]
        return remote(src, xg.at[shard, rows(b)], x_s.at[way, hop, b], x_r.at[way, hop, b], at_z(step))

    def x_arrival(way, hop, b):
        step = 1 if way == 0 else -1
        shard = (z - step * (hop + 1) + NZ) % NZ
        ref = xg.at[shard, rows(b)]
        return remote(ref, ref, x_s.at[way, hop, b], x_r.at[way, hop, b], at_z(step))

    def x_used(way, hop, b):
        return hop < 3 or (b < 2) == (way == 0)

    for b in range(4):
        for way in range(2):
            x_copy(way, 0, b).start()

    def w_copy(i, d):
        strip = lane_strip(2 * i)
        return remote(wq.at[strip, (x + d) % NX], wb.at[4 - d, strip], w_s.at[i, d - 1], w_r.at[i, 3 - d], at_x(d))

    def p_copy(x2):
        src = pwt.at[:, pl.ds(pl.multiple_of((s * NX + x2) * 256, 256), 256)]
        dst = wb.at[4, s, pl.ds(pl.multiple_of(pair_q * 64, 64), 64), :]
        return remote(src, dst, p_s.at[x2], p_r.at[pair_q], (s, pair_z * NX + x2)), src, dst

    def p_self(x2):
        return jnp.logical_and(pair_z == z, x == x2)

    for d in (1, 3, 2):
        w_copy(0, d).start()
    for x2 in range(NX):
        cp, src, dst = p_copy(x2)

        @pl.when(p_self(x2))
        def _():
            pltpu.make_async_copy(src, dst, p_r.at[pair_q]).start()

        @pl.when(jnp.logical_not(p_self(x2)))
        def _():
            cp.start()

    own_x.wait()
    row_id = lax.broadcasted_iota(jnp.int32, (8, BLK), 0)
    part = jnp.zeros((8, BLK), F32)
    for b in range(4):
        xf = xg[z, b * BLK : (b + 1) * BLK, :].astype(F32)
        sums = jnp.broadcast_to(jnp.sum(xf * xf, axis=1, keepdims=True), (BLK, BLK)).T
        part = jnp.where(row_id == b, sums[:8], part)
    ssx[0] = part

    def ssx_copy(d):
        return remote(ssx.at[0], ssx.at[4 - d], ssx_s.at[d - 1], ssx_r.at[3 - d], at_x(d))

    def ssz_copy(k):
        return remote(ssz.at[0], ssz.at[NZ - k], ssz_s.at[k - 1], ssz_r.at[NZ - 1 - k], at_z(k))

    for d in (1, 3, 2):
        ssx_copy(d).start()

    def x_forward(hop, blocks=range(4)):
        for b in blocks:
            for way in range(2):
                if x_used(way, hop, b):
                    x_arrival(way, hop, b).wait_recv()
                    if hop < 3 and x_used(way, hop + 1, b):
                        x_copy(way, hop + 1, b).start()

    def wy_copy(e, d):
        src = wb.at[d, s]
        return remote(src, src, wy_s.at[e // 2, d - 1], wy_r.at[(3 - e) // 2, d - 1], at_y(e))

    def wy_arrival(e, d):
        ref = wb.at[d, lane_strip(e)]
        return remote(ref, ref, wy_s.at[e // 2, d - 1], wy_r.at[e // 2, d - 1], at_y(e))

    def wf_copy():
        src = wb.at[4, s]
        return remote(src, src, wf_s, wf_r, at_y(2))

    def wf_arrival():
        ref = wb.at[4, lane_strip(2)]
        return remote(ref, ref, wf_s, wf_r, at_y(2))

    def wc_copy(e, d):
        src = wb.at[d, lane_strip(e)]
        return remote(src, src, wc_s.at[e, d - 1], wc_r.at[e, d - 1], sibling)

    def wc_arrival(e, d):
        ref = wb.at[d, far_strip(e)]
        return remote(ref, ref, wc_s.at[e, d - 1], wc_r.at[e, d - 1], sibling)

    def w_arrive(i, d):
        ref = wb.at[d, lane_strip(2 * i)]
        remote(ref, ref, w_s.at[i, d - 1], w_r.at[i, d - 1], at_x(d)).wait_recv()

    def w_pass(d):
        for e in (1, 3):
            wy_copy(e, d).start()
        wc_copy(0, d).start()

    x_forward(0, (0, 1))
    for d in (1, 2, 3):
        ssx_copy(d).wait_recv()
    ssz[0] = ssx[0] + ssx[1] + ssx[2] + ssx[3]
    for k in (1, 7, 2, 6, 3, 5, 4):
        ssz_copy(k).start()
    for d in (1, 3):
        w_arrive(0, d)
        w_pass(d)
    for d in (1, 3, 2):
        w_copy(1, d).start()
    x_forward(0, (2, 3))
    w_arrive(0, 2)
    w_pass(2)
    x_forward(1, (0, 1))
    for q in range(4):
        ref = wb.at[4, s, pl.ds(q * 64, 64), :]
        remote(ref, ref, p_s.at[q], p_r.at[q], sibling).wait_recv()
    w_pass(4)
    wf_copy().start()
    x_forward(1, (2, 3))

    for k in range(1, NZ):
        ssz_copy(k).wait_recv()
    total = ssz[0]
    for k in range(1, NZ):
        total = total + ssz[k]
    scale = lax.rsqrt(total * (1.0 / FEATURES) + EPS)
    for b in range(4):
        rcol[b] = jnp.broadcast_to(scale[b : b + 1, :], (BLK, BLK)).T

    def normalise(shard):
        row = (shard * NX + x) * 2
        g = jnp.concatenate([gain[pl.ds(row, 1), :], gain[pl.ds(row + 1, 1), :]], axis=1)

        def one(b, carry):
            at = pl.ds(pl.multiple_of(b * BLK, BLK), BLK)
            r = rcol[b]
            v = xg[shard, at, :].astype(F32) * jnp.concatenate([r, r], axis=1) * g
            xn[at, pl.ds(pl.multiple_of(shard * 256, 256), 256)] = v.astype(BF16)
            return carry

        lax.fori_loop(0, 4, one, 0)

    normalise(z)
    normalise((z + 1) % NZ)
    normalise((z + 7) % NZ)
    for d in (1, 3, 2):
        w_arrive(1, d)
        wc_copy(2, d).start()

    def wo_block(strip, x2):
        return wo.at[:, pl.ds(pl.multiple_of((strip * NX + x2) * 256, 256), 256)]

    own_wo = [pltpu.make_async_copy(wo_block(k, x), wob.at[0, k], local_sem.at[2 + k]) for k in range(NZ)]
    for cp in own_wo:
        cp.start()

    def o_copy(i, d):
        strip = lane_strip(2 * i)
        return remote(wo_block(strip, (x + d) % NX), wob.at[4 - d, strip], o_s.at[i, d - 1], o_r.at[i, 3 - d], at_x(d))

    def oy_copy(e):
        src = wob.at[pl.ds(1, 3), s]
        return remote(src, src, oy_s.at[e // 2], oy_r.at[(3 - e) // 2], at_y(e))

    def oy_arrival(e):
        ref = wob.at[pl.ds(1, 3), lane_strip(e)]
        return remote(ref, ref, oy_s.at[e // 2], oy_r.at[e // 2], at_y(e))

    def oc_copy(e):
        src = wob.at[pl.ds(1, 3), lane_strip(e)]
        return remote(src, src, oc_s.at[e], oc_r.at[e], sibling)

    def oc_arrival(e):
        ref = wob.at[pl.ds(1, 3), far_strip(e)]
        return remote(ref, ref, oc_s.at[e], oc_r.at[e], sibling)

    def o_arrive(i):
        strip = lane_strip(2 * i)
        for d in (1, 2, 3):
            ref = wob.at[d, strip]
            remote(ref, ref, o_s.at[i, d - 1], o_r.at[i, d - 1], at_x(d)).wait_recv()

    for d in (1, 3, 2):
        o_copy(0, d).start()

    x_forward(2)
    for d in (1, 3, 2):
        o_copy(1, d).start()
    normalise((z + 2) % NZ)
    normalise((z + 6) % NZ)
    for d in (1, 3, 2, 4):
        for e in (1, 3):
            wy_arrival(e, d).wait_recv()
            wc_copy(e, d).start()
    wf_arrival().wait_recv()
    wc_copy(2, 4).start()
    normalise((z + 3) % NZ)
    normalise((z + 5) % NZ)
    o_arrive(0)
    oy_copy(1).start()
    oy_copy(3).start()
    oc_copy(0).start()
    x_forward(3)
    normalise((z + 4) % NZ)
    for e in range(4):
        for d in range(1, 5):
            wc_arrival(e, d).wait_recv()
    own_w.wait()

    acc = nt_dot(xn[:, :256], wb[4, 0])
    for k in range(1, NZ):
        acc = acc + nt_dot(xn[:, k * 256 : (k + 1) * 256], wb[4, k])
    kvown[...] = acc.reshape(4, BLK, 256)
    kvs[...] = acc.astype(BF16).reshape(4, BLK, 256)

    def kv_copy(d):
        return remote(kvs.at[(x + d) % NX], kvr.at[3 - d], kv_s.at[d - 1], kv_r.at[3 - d], at_x(d))

    for d in (1, 3, 2):
        kv_copy(d).start()

    def q_copy(xa, d):
        return remote(qs.at[xa, (x + d) % NX], qr.at[3 - d, xa], q_s.at[xa, d - 1], q_r.at[xa, 3 - d], at_x(d))

    def q_part(d, carry):
        xa = (x + d) % NX
        a = jnp.dot(xn[...], wb[d].reshape(2048, 256), preferred_element_type=F32).reshape(4, BLK, 256)
        qs[xa] = a.astype(BF16)
        qown[xa] = a
        return carry

    lax.fori_loop(0, 4, q_part, 0)

    block = s * NX + x
    for d in (1, 2, 3):
        kv_copy(d).wait_recv()
    mine = kvown[x] + kvr[0].astype(F32) + kvr[1].astype(F32) + kvr[2].astype(F32)
    kvtab[block] = mine.astype(BF16)

    def ka_copy(d):
        return remote(kvtab.at[block], kvtab.at[block], ka_s.at[d - 1], ka_r.at[3 - d], at_x(d))

    def ka_arrival(d):
        ref = kvtab.at[s * NX + (x + d) % NX]
        return remote(ref, ref, ka_s.at[d - 1], ka_r.at[d - 1], at_x(d))

    def ky_copy(e, d):
        ref = kvtab.at[s * NX + (x + d) % NX]
        return remote(ref, ref, ky_s.at[e - 1, d], ky_r.at[3 - e, d], at_y(e))

    def ky_arrival(e, d):
        ref = kvtab.at[lane_strip(e) * NX + (x + d) % NX]
        return remote(ref, ref, ky_s.at[e - 1, d], ky_r.at[e - 1, d], at_y(e))

    def group(strip):
        return kvtab.at[pl.ds(strip * NX, NX)]

    def kc_copy(e):
        ref = group(lane_strip(e))
        return remote(ref, ref, kc_s.at[e], kc_r.at[e], sibling)

    def kc_arrival(e):
        ref = group(far_strip(e))
        return remote(ref, ref, kc_s.at[e], kc_r.at[e], sibling)

    for d in (1, 3, 2):
        ka_copy(d).start()
    for e in (1, 3, 2):
        ky_copy(e, 0).start()
    for d in (1, 3):
        ka_arrival(d).wait_recv()
        for e in (1, 3, 2):
            ky_copy(e, d).start()
    for xa in range(NX):
        for e in (1, 3, 2):
            q_copy(xa, e).start()
    ka_arrival(2).wait_recv()
    for e in (1, 3, 2):
        ky_copy(e, 2).start()
    kc_copy(0).start()

    o_arrive(1)
    oc_copy(2).start()
    for e in (1, 3):
        oy_arrival(e).wait_recv()
        oc_copy(e).start()
    for e in (1, 3, 2):
        for d in (0, 1, 3, 2):
            ky_arrival(e, d).wait_recv()
        kc_copy(e).start()

    for xa in range(NX):
        for d in (1, 2, 3):
            q_copy(xa, d).wait_recv()
        v = qown[xa, x] + qr[0, xa].astype(F32) + qr[1, xa].astype(F32) + qr[2, xa].astype(F32)
        qb[xa] = v.astype(BF16)

    for e in range(4):
        kc_arrival(e).wait_recv()

    listed = [anc[j, block] for j in range(5)]
    tables = [kvtab[jnp.maximum(i, 0)] for i in listed] + [kvtab[block]]
    causal = lax.broadcasted_iota(jnp.int32, (BLK, BLK), 0) >= lax.broadcasted_iota(jnp.int32, (BLK, BLK), 1)
    causal = jnp.concatenate([causal, causal], axis=0)
    for xa in range(NX):
        q2 = jnp.concatenate([qb[xa, :, :HD], qb[xa, :, HD:]], axis=0)
        masks, scores = [], []
        for j in range(6):
            sc = nt_dot(q2, tables[j][:, :HD]) * HD**-0.5
            ok = causal if j == 5 else jnp.broadcast_to(listed[j], (2 * BLK, BLK)) >= 0
            masks.append(ok)
            scores.append(jnp.where(ok, sc, NEG))
        top = functools.reduce(jnp.maximum, scores)
        top = jnp.max(top, axis=1, keepdims=True)
        weights = [jnp.where(ok, jnp.exp(sc - top), 0.0) for ok, sc in zip(masks, scores)]
        total = jnp.sum(functools.reduce(jnp.add, weights), axis=1, keepdims=True)
        got = jnp.zeros((2 * BLK, HD), F32)
        for j in range(6):
            got = got + jnp.dot(weights[j].astype(BF16), tables[j][:, HD:], preferred_element_type=F32)
        got = (got / total).astype(BF16)
        attb[x, xa] = jnp.concatenate([got[:BLK], got[BLK:]], axis=1)

    def half(b, h):
        return attb.at[b, pl.ds(2 * h, 2)]

    def at_copy(d, h):
        return remote(half(x, h), half(x, h), at_s.at[d // 2, h], at_r.at[(3 - d) // 2, h], at_x(d))

    def at_arrival(d, h):
        ref = half((x + d) % NX, h)
        return remote(ref, ref, at_s.at[d // 2, h], at_r.at[d // 2, h], at_x(d))

    def af_copy(d):
        h = 0 if d == 1 else 1
        ref = half((x + 4 - d) % NX, h)
        return remote(ref, ref, af_s.at[h], af_r.at[h], at_x(d))

    def af_arrival(h):
        ref = half((x + 2) % NX, h)
        return remote(ref, ref, af_s.at[h], af_r.at[h], at_x(1))

    for h in range(2):
        at_copy(1, h).start()
        at_copy(3, 1 - h).start()
    for cp in own_wo:
        cp.wait()
    for e in range(4):
        oc_arrival(e).wait_recv()

    def at_ready(d):
        if d == 1:
            at_arrival(3, 0).wait_recv()
            af_copy(1).start()
            at_arrival(1, 1).wait_recv()
            af_copy(3).start()
            at_arrival(1, 0).wait_recv()
        elif d == 3:
            at_arrival(3, 1).wait_recv()
        elif d == 2:
            af_arrival(0).wait_recv()
            af_arrival(1).wait_recv()

    order = (0, 1, 3, 2)

    def term(d, shard):
        b = (x + d) % NX
        a = jnp.dot(attb[b, x], wob[0, shard], preferred_element_type=F32)
        for e in range(1, NX):
            a = a + jnp.dot(attb[b, (x + e) % NX], wob[e, shard], preferred_element_type=F32)
        return a

    def r_copy(way, k, d, h):
        step = 1 if way == 0 else -1
        at = pl.ds(h * 64, 64)
        sem = (way, k - 1, d, h)
        return remote(
            rsend.at[way, k - 1, d, at], rrecv.at[way, k - 1, d, at], rs_s.at[sem], rs_r.at[sem], at_z(step)
        )

    def long_way(i):
        return i % 2

    def r_step(way, k, d, longest):
        step = 1 if way == 0 else -1
        v = term(d, (z + step * k + NZ) % NZ)
        for h in range(2):
            at = slice(h * 64, h * 64 + 64)
            u = v[at]
            if k < longest:
                r_copy(way, k + 1, d, h).wait_recv()
                u = u + rrecv[way, k, d, at].astype(F32)
            rsend[way, k - 1, d, at] = u.astype(BF16)
            r_copy(way, k, d, h).start()

    sent = []
    for t in range(8):
        for i, d in enumerate(order):
            stage = t - i
            if stage < 0 or stage > 4:
                continue
            far = long_way(i)
            if stage == 0:
                at_ready(d)
            if stage < 4:
                r_step(far, 4 - stage, d, 4)
                sent.append((far, 4 - stage, d))
            if stage < 3:
                r_step(1 - far, 3 - stage, d, 3)
                sent.append((1 - far, 3 - stage, d))
            if stage == 4:
                v = term(d, z)
                for h in range(2):
                    at = slice(h * 64, h * 64 + 64)
                    u = v[at]
                    for way in range(2):
                        r_copy(way, 1, d, h).wait_recv()
                        u = u + rrecv[way, 0, d, at].astype(F32)
                    out[pl.ds(pl.multiple_of(((x + d) % NX) * BLK + h * 64, 64), 64), :] = u.astype(BF16)

    for way, k, d in sent:
        r_copy(way, k, d, 0).wait_send()
        r_copy(way, k, d, 1).wait_send()
    for b in range(4):
        for way in range(2):
            for hop in range(4):
                if x_used(way, hop, b):
                    x_copy(way, hop, b).wait_send()
    for i in range(2):
        for d in (1, 2, 3):
            w_copy(i, d).wait_send()
            o_copy(i, d).wait_send()
    for x2 in range(NX):
        cp = p_copy(x2)[0]

        @pl.when(jnp.logical_not(p_self(x2)))
        def _():
            cp.wait_send()

    for d in (1, 2, 3):
        ssx_copy(d).wait_send()
        kv_copy(d).wait_send()
        ka_copy(d).wait_send()
        for xa in range(NX):
            q_copy(xa, d).wait_send()
        for e in range(4):
            ky_copy(d, e).wait_send()
    for d in (1, 3):
        af_copy(d).wait_send()
        for h in range(2):
            at_copy(d, h).wait_send()
    for k in range(1, NZ):
        ssz_copy(k).wait_send()
    wf_copy().wait_send()
    for e in (1, 3):
        for d in range(1, 5):
            wy_copy(e, d).wait_send()
        oy_copy(e).wait_send()
    for e in range(4):
        for d in range(1, 5):
            wc_copy(e, d).wait_send()
        oc_copy(e).wait_send()
        kc_copy(e).wait_send()


def local(tokens, norm_gain, query_weight, pair_weight, ancestors, out_weight):
    dma = pltpu.SemaphoreType.DMA
    any_ = pl.BlockSpec(memory_space=pl.ANY)
    vmem = pl.BlockSpec(memory_space=pltpu.VMEM)
    vm = pltpu.VMEM
    return pl.pallas_call(
        kernel,
        out_shape=jax.ShapeDtypeStruct((512, 256), BF16),
        in_specs=[pl.BlockSpec(memory_space=pltpu.SMEM), vmem, any_, any_, any_, any_],
        out_specs=vmem,
        scratch_shapes=[
            vm((8, 512, 256), BF16),
            vm((512, 2048), BF16),
            vm((4, 128, 128), F32),
            vm((4, 8, 128), F32),
            vm((8, 8, 128), F32),
            vm((5, 8, 256, 256), BF16),
            vm((4, 8, 256, 256), BF16),
            vm((4, 128, 256), BF16),
            vm((3, 128, 256), BF16),
            vm((4, 128, 256), F32),
            vm((32, 128, 256), BF16),
            vm((4, 4, 128, 256), BF16),
            vm((3, 4, 128, 256), BF16),
            vm((4, 4, 128, 256), F32),
            vm((4, 128, 256), BF16),
            vm((4, 4, 128, 256), BF16),
            vm((2, 4, 4, 128, 256), BF16),
            vm((2, 4, 4, 128, 256), BF16),
            dma((10,)),
            dma((2, 4, 4)), dma((2, 4, 4)), dma((3,)), dma((3,)), dma((7,)), dma((7,)),
            dma((2, 3)), dma((2, 3)), dma((4,)), dma((4,)), dma((2, 4)), dma((2, 4)), dma(()), dma(()), dma((4, 4)), dma((4, 4)),
            dma((2, 3)), dma((2, 3)), dma((2,)), dma((2,)), dma((4,)), dma((4,)),
            dma((3,)), dma((3,)), dma((3,)), dma((3,)), dma((3, 4)), dma((3, 4)), dma((4,)), dma((4,)),
            dma((4, 3)), dma((4, 3)), dma((2, 2)), dma((2, 2)), dma((2,)), dma((2,)), dma((2, 4, 4, 2)), dma((2, 4, 4, 2)),
        ],
        compiler_params=pltpu.CompilerParams(collective_id=0, has_side_effects=True, vmem_limit_bytes=60 << 20),
        cost_estimate=pl.CostEstimate(flops=6 * 10**9, bytes_accessed=10 << 20, transcendentals=10**6),
        name="tree_attention",
    )(
        ancestors.T,
        norm_gain.reshape(64, 128),
        tokens,
        query_weight.reshape(8, 4, 256, 256),
        pair_weight.T,
        out_weight,
    )


def solution(mesh):
    return jax.shard_map(
        local,
        mesh=mesh,
        in_specs=(P("seq", "mp"), P(), P(None, "mp"), P(None, "mp"), P(), P("mp", None)),
        out_specs=P("seq", "mp"),
        check_vma=False,
    )
```

```python
import functools

import jax
import jax.numpy as jnp
from jax import lax
from jax.experimental import pallas as pl
from jax.experimental.pallas import tpu as pltpu
from jax.sharding import PartitionSpec as P

MESH = pl.DeviceIdType.MESH
HD = 128
BLK = 128
NX, NY, NZ = 4, 4, 8
FEATURES = 8192
EPS = 1e-05
NEG = -1e30
F32 = jnp.float32
BF16 = jnp.bfloat16


def nt_dot(a, b):
    return lax.dot_general(a, b, (((1,), (1,)), ((), ())), preferred_element_type=F32)


def kernel(
    anc, gain, tok, wq, pwt, wo, out,
    xg, xn, rcol, ssx, ssz, wb, wob, kvs, kvr, kvown, kvtab, qs, qr, qown, qb, attb, rsend, rrecv,
    local_sem, x_s, x_r, ssx_s, ssx_r, ssz_s, ssz_r,
    w_s, w_r, p_s, p_r, wy_s, wy_r, wf_s, wf_r, wc_s, wc_r,
    o_s, o_r, oy_s, oy_r, oc_s, oc_r,
    kv_s, kv_r, ka_s, ka_r, ky_s, ky_r, kf_s, kf_r, kc_s, kc_r, q_s, q_r, at_s, at_r, af_s, af_r, rs_s, rs_r,
):
    s = lax.axis_index("seq")
    m = lax.axis_index("mp")
    y, c = s // 2, s % 2
    z, x = m // NX, m % NX

    def at_x(d):
        return (s, z * NX + (x + d) % NX)

    def at_z(k):
        return (s, ((z + k + NZ) % NZ) * NX + x)

    def at_y(e):
        return (((y + e) % NY) * 2 + c, m)

    sibling = (y * 2 + 1 - c, m)

    def lane_strip(e):
        return ((y + e) % NY) * 2 + c

    def far_strip(e):
        return ((y + e) % NY) * 2 + 1 - c

    def remote(src, dst, ss, rs, dev):
        return pltpu.make_async_remote_copy(
            src_ref=src, dst_ref=dst, send_sem=ss, recv_sem=rs, device_id=dev, device_id_type=MESH
        )

    pair_q = (m // 16) * 2 + m % 2
    pair_z = (m // 2) % NZ

    barrier = pltpu.get_barrier_semaphore()
    peers = [at_x(d) for d in (1, 2, 3)] + [at_z(k) for k in range(1, NZ)] + [at_y(e) for e in (1, 2, 3)] + [sibling]
    for dev in peers:
        pl.semaphore_signal(barrier, inc=1, device_id=dev, device_id_type=MESH)
    for source in (2 * z, 2 * z + 1, 16 + 2 * z, 17 + 2 * z):

        @pl.when(source != m)
        def _():
            pl.semaphore_signal(barrier, inc=1, device_id=(s, source), device_id_type=MESH)

    own_x = pltpu.make_async_copy(tok, xg.at[z], local_sem.at[0])
    own_x.start()
    own_w = pltpu.make_async_copy(wq.at[:, x], wb.at[0], local_sem.at[1])
    own_w.start()
    pl.semaphore_wait(barrier, len(peers) + jnp.where(pair_z == z, 3, 4))

    def rows(b):
        return pl.ds(b * BLK, BLK)

    def x_copy(way, hop, b):
        step = 1 if way == 0 else -1
        shard = (z - step * hop + NZ) % NZ
        src = tok.at[rows(b)] if hop == 0 else xg.at[shard, rows(b)]
        return remote(src, xg.at[shard, rows(b)], x_s.at[way, hop, b], x_r.at[way, hop, b], at_z(step))

    def x_arrival(way, hop, b):
        step = 1 if way == 0 else -1
        shard = (z - step * (hop + 1) + NZ) % NZ
        ref = xg.at[shard, rows(b)]
        return remote(ref, ref, x_s.at[way, hop, b], x_r.at[way, hop, b], at_z(step))

    def x_used(way, hop, b):
        return hop < 3 or (b < 2) == (way == 0)

    for b in range(4):
        for way in range(2):
            x_copy(way, 0, b).start()

    def w_copy(i, d):
        strip = lane_strip(2 * i)
        return remote(wq.at[strip, (x + d) % NX], wb.at[4 - d, strip], w_s.at[i, d - 1], w_r.at[i, 3 - d], at_x(d))

    def p_copy(x2):
        src = pwt.at[:, pl.ds(pl.multiple_of((s * NX + x2) * 256, 256), 256)]
        dst = wb.at[4, s, pl.ds(pl.multiple_of(pair_q * 64, 64), 64), :]
        return remote(src, dst, p_s.at[x2], p_r.at[pair_q], (s, pair_z * NX + x2)), src, dst

    def p_self(x2):
        return jnp.logical_and(pair_z == z, x == x2)

    for d in (1, 3, 2):
        w_copy(0, d).start()
    for x2 in range(NX):
        cp, src, dst = p_copy(x2)

        @pl.when(p_self(x2))
        def _():
            pltpu.make_async_copy(src, dst, p_r.at[pair_q]).start()

        @pl.when(jnp.logical_not(p_self(x2)))
        def _():
            cp.start()

    own_x.wait()
    row_id = lax.broadcasted_iota(jnp.int32, (8, BLK), 0)
    part = jnp.zeros((8, BLK), F32)
    for b in range(4):
        xf = xg[z, b * BLK : (b + 1) * BLK, :].astype(F32)
        sums = jnp.broadcast_to(jnp.sum(xf * xf, axis=1, keepdims=True), (BLK, BLK)).T
        part = jnp.where(row_id == b, sums[:8], part)
    ssx[0] = part

    def ssx_copy(d):
        return remote(ssx.at[0], ssx.at[4 - d], ssx_s.at[d - 1], ssx_r.at[3 - d], at_x(d))

    def ssz_copy(k):
        return remote(ssz.at[0], ssz.at[NZ - k], ssz_s.at[k - 1], ssz_r.at[NZ - 1 - k], at_z(k))

    for d in (1, 3, 2):
        ssx_copy(d).start()

    def x_forward(hop, blocks=range(4)):
        for b in blocks:
            for way in range(2):
                if x_used(way, hop, b):
                    x_arrival(way, hop, b).wait_recv()
                    if hop < 3 and x_used(way, hop + 1, b):
                        x_copy(way, hop + 1, b).start()

    def wy_copy(e, d):
        src = wb.at[d, s]
        return remote(src, src, wy_s.at[e // 2, d - 1], wy_r.at[(3 - e) // 2, d - 1], at_y(e))

    def wy_arrival(e, d):
        ref = wb.at[d, lane_strip(e)]
        return remote(ref, ref, wy_s.at[e // 2, d - 1], wy_r.at[e // 2, d - 1], at_y(e))

    def wf_copy():
        src = wb.at[4, s]
        return remote(src, src, wf_s, wf_r, at_y(2))

    def wf_arrival():
        ref = wb.at[4, lane_strip(2)]
        return remote(ref, ref, wf_s, wf_r, at_y(2))

    def wc_copy(e, d):
        src = wb.at[d, lane_strip(e)]
        return remote(src, src, wc_s.at[e, d - 1], wc_r.at[e, d - 1], sibling)

    def wc_arrival(e, d):
        ref = wb.at[d, far_strip(e)]
        return remote(ref, ref, wc_s.at[e, d - 1], wc_r.at[e, d - 1], sibling)

    def w_arrive(i, d):
        ref = wb.at[d, lane_strip(2 * i)]
        remote(ref, ref, w_s.at[i, d - 1], w_r.at[i, d - 1], at_x(d)).wait_recv()

    def w_pass(d):
        for e in (1, 3):
            wy_copy(e, d).start()
        wc_copy(0, d).start()

    x_forward(0, (0, 1))
    for d in (1, 2, 3):
        ssx_copy(d).wait_recv()
    ssz[0] = ssx[0] + ssx[1] + ssx[2] + ssx[3]
    for k in (1, 7, 2, 6, 3, 5, 4):
        ssz_copy(k).start()
    for d in (1, 3):
        w_arrive(0, d)
        w_pass(d)
    for d in (1, 3, 2):
        w_copy(1, d).start()
    x_forward(0, (2, 3))
    w_arrive(0, 2)
    w_pass(2)
    def wo_block(strip, x2):
        return wo.at[:, pl.ds(pl.multiple_of((strip * NX + x2) * 256, 256), 256)]

    own_wo = [pltpu.make_async_copy(wo_block(k, x), wob.at[0, k], local_sem.at[2 + k]) for k in range(NZ)]
    for cp in own_wo:
        cp.start()

    def o_copy(i, d):
        strip = lane_strip(2 * i)
        return remote(wo_block(strip, (x + d) % NX), wob.at[4 - d, strip], o_s.at[i, d - 1], o_r.at[i, 3 - d], at_x(d))

    def oy_copy(e):
        src = wob.at[pl.ds(1, 3), s]
        return remote(src, src, oy_s.at[e // 2], oy_r.at[(3 - e) // 2], at_y(e))

    def oy_arrival(e):
        ref = wob.at[pl.ds(1, 3), lane_strip(e)]
        return remote(ref, ref, oy_s.at[e // 2], oy_r.at[e // 2], at_y(e))

    def oc_copy(e):
        src = wob.at[pl.ds(1, 3), lane_strip(e)]
        return remote(src, src, oc_s.at[e], oc_r.at[e], sibling)

    def oc_arrival(e):
        ref = wob.at[pl.ds(1, 3), far_strip(e)]
        return remote(ref, ref, oc_s.at[e], oc_r.at[e], sibling)

    def o_arrive(i):
        strip = lane_strip(2 * i)
        for d in (1, 2, 3):
            ref = wob.at[d, strip]
            remote(ref, ref, o_s.at[i, d - 1], o_r.at[i, d - 1], at_x(d)).wait_recv()

    x_forward(1)
    for q in range(4):
        ref = wb.at[4, s, pl.ds(q * 64, 64), :]
        remote(ref, ref, p_s.at[q], p_r.at[q], sibling).wait_recv()
    w_pass(4)
    wf_copy().start()
    for d in (1, 3, 2):
        w_arrive(1, d)
        wc_copy(2, d).start()
    for d in (1, 3, 2):
        o_copy(0, d).start()
    x_forward(2)
    for d in (1, 3, 2):
        o_copy(1, d).start()

    for k in range(1, NZ):
        ssz_copy(k).wait_recv()
    total = ssz[0]
    for k in range(1, NZ):
        total = total + ssz[k]
    scale = lax.rsqrt(total * (1.0 / FEATURES) + EPS)
    for b in range(4):
        rcol[b] = jnp.broadcast_to(scale[b : b + 1, :], (BLK, BLK)).T

    def normalise(shard):
        row = (shard * NX + x) * 2
        g = jnp.concatenate([gain[pl.ds(row, 1), :], gain[pl.ds(row + 1, 1), :]], axis=1)

        def one(b, carry):
            at = pl.ds(pl.multiple_of(b * BLK, BLK), BLK)
            r = rcol[b]
            v = xg[shard, at, :].astype(F32) * jnp.concatenate([r, r], axis=1) * g
            xn[at, pl.ds(pl.multiple_of(shard * 256, 256), 256)] = v.astype(BF16)
            return carry

        lax.fori_loop(0, 4, one, 0)

    normalise(z)
    normalise((z + 1) % NZ)
    normalise((z + 7) % NZ)
    normalise((z + 2) % NZ)
    normalise((z + 6) % NZ)
    for d in (1, 3, 2, 4):
        for e in (1, 3):
            wy_arrival(e, d).wait_recv()
            wc_copy(e, d).start()
    wf_arrival().wait_recv()
    wc_copy(2, 4).start()
    normalise((z + 3) % NZ)
    normalise((z + 5) % NZ)
    x_forward(3)
    normalise((z + 4) % NZ)
    for e in range(4):
        wc_arrival(e, 4).wait_recv()

    acc = nt_dot(xn[:, :256], wb[4, 0])
    for k in range(1, NZ):
        acc = acc + nt_dot(xn[:, k * 256 : (k + 1) * 256], wb[4, k])
    kvown[...] = acc.reshape(4, BLK, 256)
    kvs[...] = acc.astype(BF16).reshape(4, BLK, 256)

    def kv_copy(d):
        return remote(kvs.at[(x + d) % NX], kvr.at[3 - d], kv_s.at[d - 1], kv_r.at[3 - d], at_x(d))

    for d in (1, 3, 2):
        kv_copy(d).start()

    o_arrive(0)
    oy_copy(1).start()
    oy_copy(3).start()
    oc_copy(0).start()

    block = s * NX + x
    for d in (1, 3, 2):
        kv_copy(d).wait_recv()
    mine = kvown[x] + kvr[0].astype(F32) + kvr[1].astype(F32) + kvr[2].astype(F32)
    kvtab[block] = mine.astype(BF16)

    def ka_copy(d):
        return remote(kvtab.at[block], kvtab.at[block], ka_s.at[d - 1], ka_r.at[3 - d], at_x(d))

    def ka_arrival(d):
        ref = kvtab.at[s * NX + (x + d) % NX]
        return remote(ref, ref, ka_s.at[d - 1], ka_r.at[d - 1], at_x(d))

    def ky_copy(e, d):
        ref = kvtab.at[s * NX + (x + d) % NX]
        return remote(ref, ref, ky_s.at[e // 2, d], ky_r.at[(3 - e) // 2, d], at_y(e))

    def ky_arrival(e, d):
        ref = kvtab.at[lane_strip(e) * NX + (x + d) % NX]
        return remote(ref, ref, ky_s.at[e // 2, d], ky_r.at[e // 2, d], at_y(e))

    def kf_half(strip, d, i):
        return kvtab.at[strip * NX + (x + d) % NX, pl.ds((1 - i) * 64, 64)]

    def kf_copy(e, d):
        ref = kf_half(lane_strip(e), d, e // 2)
        return remote(ref, ref, kf_s.at[e // 2, d], kf_r.at[e // 2, d], at_y(4 - e))

    def kf_arrival(i, d):
        ref = kf_half(lane_strip(2), d, i)
        return remote(ref, ref, kf_s.at[i, d], kf_r.at[i, d], at_y(1))

    def group(strip):
        return kvtab.at[pl.ds(strip * NX, NX)]

    def kc_copy(e):
        ref = group(lane_strip(e))
        return remote(ref, ref, kc_s.at[e], kc_r.at[e], sibling)

    def kc_arrival(e):
        ref = group(far_strip(e))
        return remote(ref, ref, kc_s.at[e], kc_r.at[e], sibling)

    def ky_pass(d):
        for e in (1, 3):
            ky_arrival(e, d).wait_recv()
            kf_copy(e, d).start()

    for d in (1, 3, 2):
        ka_copy(d).start()
    for e in (1, 3):
        ky_copy(e, 0).start()

    def q_copy(xa, d):
        return remote(qs.at[xa, (x + d) % NX], qr.at[3 - d, xa], q_s.at[xa, d - 1], q_r.at[xa, 3 - d], at_x(d))

    def q_part(d, carry):
        xa = (x + d) % NX
        a = jnp.dot(xn[...], wb[d].reshape(2048, 256), preferred_element_type=F32).reshape(4, BLK, 256)
        qs[xa] = a.astype(BF16)
        qown[xa] = a
        for e in (1, 3, 2):
            q_copy(xa, e).start()
        return carry

    own_w.wait()
    for e in range(4):
        for d in range(1, 4):
            wc_arrival(e, d).wait_recv()
    lax.fori_loop(0, 4, q_part, 0)

    for d in (1, 3):
        ka_arrival(d).wait_recv()
        for e in (1, 3):
            ky_copy(e, d).start()
    ky_pass(0)
    ka_arrival(2).wait_recv()
    for e in (1, 3):
        ky_copy(e, 2).start()
    kc_copy(0).start()
    for d in (1, 3):
        ky_pass(d)
    o_arrive(1)
    oc_copy(2).start()
    for e in (1, 3):
        oy_arrival(e).wait_recv()
        oc_copy(e).start()
    ky_pass(2)
    kc_copy(1).start()
    kc_copy(3).start()
    for d in (0, 1, 3, 2):
        for i in range(2):
            kf_arrival(i, d).wait_recv()
    kc_copy(2).start()

    for xa in range(NX):
        for d in (1, 2, 3):
            q_copy(xa, d).wait_recv()
        v = qown[xa, x] + qr[0, xa].astype(F32) + qr[1, xa].astype(F32) + qr[2, xa].astype(F32)
        qb[xa] = v.astype(BF16)

    for e in range(4):
        kc_arrival(e).wait_recv()

    listed = [anc[j, block] for j in range(5)]
    tables = [kvtab[jnp.maximum(i, 0)] for i in listed] + [kvtab[block]]
    causal = lax.broadcasted_iota(jnp.int32, (BLK, BLK), 0) >= lax.broadcasted_iota(jnp.int32, (BLK, BLK), 1)
    causal = jnp.concatenate([causal, causal], axis=0)
    for xa in range(NX):
        q2 = jnp.concatenate([qb[xa, :, :HD], qb[xa, :, HD:]], axis=0)
        masks, scores = [], []
        for j in range(6):
            sc = nt_dot(q2, tables[j][:, :HD]) * HD**-0.5
            ok = causal if j == 5 else jnp.broadcast_to(listed[j], (2 * BLK, BLK)) >= 0
            masks.append(ok)
            scores.append(jnp.where(ok, sc, NEG))
        top = functools.reduce(jnp.maximum, scores)
        top = jnp.max(top, axis=1, keepdims=True)
        weights = [jnp.where(ok, jnp.exp(sc - top), 0.0) for ok, sc in zip(masks, scores)]
        total = jnp.sum(functools.reduce(jnp.add, weights), axis=1, keepdims=True)
        got = jnp.zeros((2 * BLK, HD), F32)
        for j in range(6):
            got = got + jnp.dot(weights[j].astype(BF16), tables[j][:, HD:], preferred_element_type=F32)
        got = (got / total).astype(BF16)
        attb[x, xa] = jnp.concatenate([got[:BLK], got[BLK:]], axis=1)

    def half(b, h):
        return attb.at[b, pl.ds(2 * h, 2)]

    def at_copy(d, h):
        return remote(half(x, h), half(x, h), at_s.at[d // 2, h], at_r.at[(3 - d) // 2, h], at_x(d))

    def at_arrival(d, h):
        ref = half((x + d) % NX, h)
        return remote(ref, ref, at_s.at[d // 2, h], at_r.at[d // 2, h], at_x(d))

    def af_copy(d):
        h = 0 if d == 1 else 1
        ref = half((x + 4 - d) % NX, h)
        return remote(ref, ref, af_s.at[h], af_r.at[h], at_x(d))

    def af_arrival(h):
        ref = half((x + 2) % NX, h)
        return remote(ref, ref, af_s.at[h], af_r.at[h], at_x(1))

    for h in range(2):
        at_copy(1, h).start()
        at_copy(3, 1 - h).start()
    for cp in own_wo:
        cp.wait()
    for e in range(4):
        oc_arrival(e).wait_recv()

    def at_ready(d):
        if d == 1:
            at_arrival(3, 0).wait_recv()
            af_copy(1).start()
            at_arrival(1, 1).wait_recv()
            af_copy(3).start()
            at_arrival(1, 0).wait_recv()
        elif d == 3:
            at_arrival(3, 1).wait_recv()
        elif d == 2:
            af_arrival(0).wait_recv()
            af_arrival(1).wait_recv()

    def term(d, shard):
        b = (x + d) % NX
        a = jnp.dot(attb[b, x], wob[0, shard], preferred_element_type=F32)
        for e in range(1, NX):
            a = a + jnp.dot(attb[b, (x + e) % NX], wob[e, shard], preferred_element_type=F32)
        return a

    def r_copy(way, k, d, h):
        step = 1 if way == 0 else -1
        at = pl.ds(h * 64, 64)
        sem = (way, k - 1, d, h)
        return remote(
            rsend.at[way, k - 1, d, at], rrecv.at[way, k - 1, d, at], rs_s.at[sem], rs_r.at[sem], at_z(step)
        )

    long_way = {0: 0, 1: 1, 3: 0, 2: 1}

    def r_step(way, k, d, longest):
        step = 1 if way == 0 else -1
        v = term(d, (z + step * k + NZ) % NZ)
        for h in range(2):
            at = slice(h * 64, h * 64 + 64)
            u = v[at]
            if k < longest:
                r_copy(way, k + 1, d, h).wait_recv()
                u = u + rrecv[way, k, d, at].astype(F32)
            rsend[way, k - 1, d, at] = u.astype(BF16)
            r_copy(way, k, d, h).start()

    sent = []
    schedule = (
        (0, 0), (1, 0), (0, 1), (0, 3), (2, 0), (0, 2), (1, 1), (1, 3), (3, 0), (1, 2),
        (2, 1), (2, 3), (4, 0), (2, 2), (3, 1), (3, 3), (3, 2), (4, 1), (4, 3), (4, 2),
    )
    for stage, d in schedule:
        far = long_way[d]
        if stage == 0:
            at_ready(d)
        if stage < 4:
            r_step(far, 4 - stage, d, 4)
            sent.append((far, 4 - stage, d))
        if stage < 3:
            r_step(1 - far, 3 - stage, d, 3)
            sent.append((1 - far, 3 - stage, d))
        if stage == 4:
            v = term(d, z)
            for h in range(2):
                at = slice(h * 64, h * 64 + 64)
                u = v[at]
                for way in range(2):
                    r_copy(way, 1, d, h).wait_recv()
                    u = u + rrecv[way, 0, d, at].astype(F32)
                out[pl.ds(pl.multiple_of(((x + d) % NX) * BLK + h * 64, 64), 64), :] = u.astype(BF16)

    for way, k, d in sent:
        r_copy(way, k, d, 0).wait_send()
        r_copy(way, k, d, 1).wait_send()
    for b in range(4):
        for way in range(2):
            for hop in range(4):
                if x_used(way, hop, b):
                    x_copy(way, hop, b).wait_send()
    for i in range(2):
        for d in (1, 2, 3):
            w_copy(i, d).wait_send()
            o_copy(i, d).wait_send()
    for x2 in range(NX):
        cp = p_copy(x2)[0]

        @pl.when(jnp.logical_not(p_self(x2)))
        def _():
            cp.wait_send()

    for d in (1, 2, 3):
        ssx_copy(d).wait_send()
        kv_copy(d).wait_send()
        ka_copy(d).wait_send()
        for xa in range(NX):
            q_copy(xa, d).wait_send()
    for d in (1, 3):
        af_copy(d).wait_send()
        for h in range(2):
            at_copy(d, h).wait_send()
    for k in range(1, NZ):
        ssz_copy(k).wait_send()
    wf_copy().wait_send()
    for e in (1, 3):
        for d in range(4):
            ky_copy(e, d).wait_send()
            kf_copy(e, d).wait_send()
    for e in (1, 3):
        for d in range(1, 5):
            wy_copy(e, d).wait_send()
        oy_copy(e).wait_send()
    for e in range(4):
        for d in range(1, 5):
            wc_copy(e, d).wait_send()
        oc_copy(e).wait_send()
        kc_copy(e).wait_send()


def local(tokens, norm_gain, query_weight, pair_weight, ancestors, out_weight):
    dma = pltpu.SemaphoreType.DMA
    any_ = pl.BlockSpec(memory_space=pl.ANY)
    vmem = pl.BlockSpec(memory_space=pltpu.VMEM)
    vm = pltpu.VMEM
    return pl.pallas_call(
        kernel,
        out_shape=jax.ShapeDtypeStruct((512, 256), BF16),
        in_specs=[pl.BlockSpec(memory_space=pltpu.SMEM), vmem, any_, any_, any_, any_],
        out_specs=vmem,
        scratch_shapes=[
            vm((8, 512, 256), BF16),
            vm((512, 2048), BF16),
            vm((4, 128, 128), F32),
            vm((4, 8, 128), F32),
            vm((8, 8, 128), F32),
            vm((5, 8, 256, 256), BF16),
            vm((4, 8, 256, 256), BF16),
            vm((4, 128, 256), BF16),
            vm((3, 128, 256), BF16),
            vm((4, 128, 256), F32),
            vm((32, 128, 256), BF16),
            vm((4, 4, 128, 256), BF16),
            vm((3, 4, 128, 256), BF16),
            vm((4, 4, 128, 256), F32),
            vm((4, 128, 256), BF16),
            vm((4, 4, 128, 256), BF16),
            vm((2, 4, 4, 128, 256), BF16),
            vm((2, 4, 4, 128, 256), BF16),
            dma((10,)),
            dma((2, 4, 4)), dma((2, 4, 4)), dma((3,)), dma((3,)), dma((7,)), dma((7,)),
            dma((2, 3)), dma((2, 3)), dma((4,)), dma((4,)), dma((2, 4)), dma((2, 4)), dma(()), dma(()), dma((4, 4)), dma((4, 4)),
            dma((2, 3)), dma((2, 3)), dma((2,)), dma((2,)), dma((4,)), dma((4,)),
            dma((3,)), dma((3,)), dma((3,)), dma((3,)), dma((2, 4)), dma((2, 4)), dma((2, 4)), dma((2, 4)), dma((4,)), dma((4,)),
            dma((4, 3)), dma((4, 3)), dma((2, 2)), dma((2, 2)), dma((2,)), dma((2,)), dma((2, 4, 4, 2)), dma((2, 4, 4, 2)),
        ],
        compiler_params=pltpu.CompilerParams(collective_id=0, has_side_effects=True, vmem_limit_bytes=60 << 20),
        cost_estimate=pl.CostEstimate(flops=6 * 10**9, bytes_accessed=10 << 20, transcendentals=10**6),
        name="tree_attention",
    )(
        ancestors.T,
        norm_gain.reshape(64, 128),
        tokens,
        query_weight.reshape(8, 4, 256, 256),
        pair_weight.T,
        out_weight,
    )


def solution(mesh):
    return jax.shard_map(
        local,
        mesh=mesh,
        in_specs=(P("seq", "mp"), P(), P(None, "mp"), P(None, "mp"), P(), P("mp", None)),
        out_specs=P("seq", "mp"),
        check_vma=False,
    )
```

```python
import functools

import jax
import jax.numpy as jnp
from jax import lax
from jax.experimental import pallas as pl
from jax.experimental.pallas import tpu as pltpu
from jax.sharding import PartitionSpec as P

MESH = pl.DeviceIdType.MESH
HD = 128
BLK = 128
NX, NY, NZ = 4, 4, 8
FEATURES = 8192
EPS = 1e-05
NEG = -1e30
F32 = jnp.float32
BF16 = jnp.bfloat16


def nt_dot(a, b):
    return lax.dot_general(a, b, (((1,), (1,)), ((), ())), preferred_element_type=F32)


def kernel(
    anc, gain, tok, wq, pwt, wo, out,
    xg, xn, rcol, ssx, ssz, wb, wob, kvs, kvr, kvown, kvtab, qs, qr, qown, qb, attb, rsend, rrecv,
    local_sem, x_s, x_r, ssx_s, ssx_r, ssz_s, ssz_r,
    w_s, w_r, p_s, p_r, wy_s, wy_r, wf_s, wf_r, wc_s, wc_r,
    o_s, o_r, oy_s, oy_r, oc_s, oc_r,
    kv_s, kv_r, ka_s, ka_r, ky_s, ky_r, kf_s, kf_r, kc_s, kc_r, q_s, q_r, at_s, at_r, af_s, af_r, rs_s, rs_r,
):
    s = lax.axis_index("seq")
    m = lax.axis_index("mp")
    y, c = s // 2, s % 2
    z, x = m // NX, m % NX

    def at_x(d):
        return (s, z * NX + (x + d) % NX)

    def at_z(k):
        return (s, ((z + k + NZ) % NZ) * NX + x)

    def at_y(e):
        return (((y + e) % NY) * 2 + c, m)

    sibling = (y * 2 + 1 - c, m)

    def lane_strip(e):
        return ((y + e) % NY) * 2 + c

    def far_strip(e):
        return ((y + e) % NY) * 2 + 1 - c

    def remote(src, dst, ss, rs, dev):
        return pltpu.make_async_remote_copy(
            src_ref=src, dst_ref=dst, send_sem=ss, recv_sem=rs, device_id=dev, device_id_type=MESH
        )

    pair_q = (m // 16) * 2 + m % 2
    pair_z = (m // 2) % NZ

    barrier = pltpu.get_barrier_semaphore()
    peers = [at_x(d) for d in (1, 2, 3)] + [at_z(k) for k in range(1, NZ)] + [at_y(e) for e in (1, 2, 3)] + [sibling]
    for dev in peers:
        pl.semaphore_signal(barrier, inc=1, device_id=dev, device_id_type=MESH)
    for source in (2 * z, 2 * z + 1, 16 + 2 * z, 17 + 2 * z):

        @pl.when(source != m)
        def _():
            pl.semaphore_signal(barrier, inc=1, device_id=(s, source), device_id_type=MESH)

    own_x = pltpu.make_async_copy(tok, xg.at[z], local_sem.at[0])
    own_x.start()
    own_w = pltpu.make_async_copy(wq.at[:, x], wb.at[0], local_sem.at[1])
    own_w.start()
    pl.semaphore_wait(barrier, len(peers) + jnp.where(pair_z == z, 3, 4))

    def rows(b):
        return pl.ds(b * BLK, BLK)

    def x_copy(way, hop, b):
        step = 1 if way == 0 else -1
        shard = (z - step * hop + NZ) % NZ
        src = tok.at[rows(b)] if hop == 0 else xg.at[shard, rows(b)]
        return remote(src, xg.at[shard, rows(b)], x_s.at[way, hop, b], x_r.at[way, hop, b], at_z(step))

    def x_arrival(way, hop, b):
        step = 1 if way == 0 else -1
        shard = (z - step * (hop + 1) + NZ) % NZ
        ref = xg.at[shard, rows(b)]
        return remote(ref, ref, x_s.at[way, hop, b], x_r.at[way, hop, b], at_z(step))

    def x_used(way, hop, b):
        return hop < 3 or (b < 2) == (way == 0)

    for b in range(2):
        for way in range(2):
            x_copy(way, 0, b).start()

    def w_copy(i, d):
        strip = lane_strip(2 * i)
        return remote(wq.at[strip, (x + d) % NX], wb.at[4 - d, strip], w_s.at[i, d - 1], w_r.at[i, 3 - d], at_x(d))

    def p_copy(x2):
        src = pwt.at[:, pl.ds(pl.multiple_of((s * NX + x2) * 256, 256), 256)]
        dst = wb.at[4, s, pl.ds(pl.multiple_of(pair_q * 64, 64), 64), :]
        return remote(src, dst, p_s.at[x2], p_r.at[pair_q], (s, pair_z * NX + x2)), src, dst

    def p_self(x2):
        return jnp.logical_and(pair_z == z, x == x2)

    for x2 in range(NX):
        cp, src, dst = p_copy(x2)

        @pl.when(p_self(x2))
        def _():
            pltpu.make_async_copy(src, dst, p_r.at[pair_q]).start()

        @pl.when(jnp.logical_not(p_self(x2)))
        def _():
            cp.start()

    for d in (1, 3, 2):
        w_copy(0, d).start()
    for b in range(2, 4):
        for way in range(2):
            x_copy(way, 0, b).start()

    own_x.wait()
    row_id = lax.broadcasted_iota(jnp.int32, (8, BLK), 0)
    part = jnp.zeros((8, BLK), F32)
    for b in range(4):
        xf = xg[z, b * BLK : (b + 1) * BLK, :].astype(F32)
        sums = jnp.broadcast_to(jnp.sum(xf * xf, axis=1, keepdims=True), (BLK, BLK)).T
        part = jnp.where(row_id == b, sums[:8], part)
    ssx[0] = part

    def ssx_copy(d):
        return remote(ssx.at[0], ssx.at[4 - d], ssx_s.at[d - 1], ssx_r.at[3 - d], at_x(d))

    def ssz_copy(k):
        return remote(ssz.at[0], ssz.at[NZ - k], ssz_s.at[k - 1], ssz_r.at[NZ - 1 - k], at_z(k))

    for d in (1, 3, 2):
        ssx_copy(d).start()

    def x_forward(hop, blocks=range(4)):
        for b in blocks:
            for way in range(2):
                if x_used(way, hop, b):
                    x_arrival(way, hop, b).wait_recv()
                    if hop < 3 and x_used(way, hop + 1, b):
                        x_copy(way, hop + 1, b).start()

    def wy_copy(e, d):
        src = wb.at[d, s]
        return remote(src, src, wy_s.at[e // 2, d - 1], wy_r.at[(3 - e) // 2, d - 1], at_y(e))

    def wy_arrival(e, d):
        ref = wb.at[d, lane_strip(e)]
        return remote(ref, ref, wy_s.at[e // 2, d - 1], wy_r.at[e // 2, d - 1], at_y(e))

    def wf_copy():
        src = wb.at[4, s]
        return remote(src, src, wf_s, wf_r, at_y(2))

    def wf_arrival():
        ref = wb.at[4, lane_strip(2)]
        return remote(ref, ref, wf_s, wf_r, at_y(2))

    def wc_copy(e, d):
        src = wb.at[d, lane_strip(e)]
        return remote(src, src, wc_s.at[e, d - 1], wc_r.at[e, d - 1], sibling)

    def wc_arrival(e, d):
        ref = wb.at[d, far_strip(e)]
        return remote(ref, ref, wc_s.at[e, d - 1], wc_r.at[e, d - 1], sibling)

    def w_arrive(i, d):
        ref = wb.at[d, lane_strip(2 * i)]
        remote(ref, ref, w_s.at[i, d - 1], w_r.at[i, d - 1], at_x(d)).wait_recv()

    def w_pass(d):
        for e in (1, 3):
            wy_copy(e, d).start()
        wc_copy(0, d).start()

    x_forward(0, (0, 1))
    for d in (1, 2, 3):
        ssx_copy(d).wait_recv()
    ssz[0] = ssx[0] + ssx[1] + ssx[2] + ssx[3]
    for k in (1, 7, 2, 6, 3, 5, 4):
        ssz_copy(k).start()
    for d in (1, 3):
        w_arrive(0, d)
        w_pass(d)
    for d in (1, 3, 2):
        w_copy(1, d).start()
    x_forward(0, (2, 3))

    def wo_block(strip, x2):
        return wo.at[:, pl.ds(pl.multiple_of((strip * NX + x2) * 256, 256), 256)]

    own_wo = [pltpu.make_async_copy(wo_block(k, x), wob.at[0, k], local_sem.at[2 + k]) for k in range(NZ)]
    for cp in own_wo:
        cp.start()

    def o_copy(i, d):
        strip = lane_strip(2 * i)
        return remote(wo_block(strip, (x + d) % NX), wob.at[4 - d, strip], o_s.at[i, d - 1], o_r.at[i, 3 - d], at_x(d))

    def oy_copy(e):
        src = wob.at[pl.ds(1, 3), s]
        return remote(src, src, oy_s.at[e // 2], oy_r.at[(3 - e) // 2], at_y(e))

    def oy_arrival(e):
        ref = wob.at[pl.ds(1, 3), lane_strip(e)]
        return remote(ref, ref, oy_s.at[e // 2], oy_r.at[e // 2], at_y(e))

    def oc_copy(e):
        src = wob.at[pl.ds(1, 3), lane_strip(e)]
        return remote(src, src, oc_s.at[e], oc_r.at[e], sibling)

    def oc_arrival(e):
        ref = wob.at[pl.ds(1, 3), far_strip(e)]
        return remote(ref, ref, oc_s.at[e], oc_r.at[e], sibling)

    def o_arrive(i):
        strip = lane_strip(2 * i)
        for d in (1, 2, 3):
            ref = wob.at[d, strip]
            remote(ref, ref, o_s.at[i, d - 1], o_r.at[i, d - 1], at_x(d)).wait_recv()

    x_forward(1, (0, 1))
    for q in range(4):
        ref = wb.at[4, s, pl.ds(q * 64, 64), :]
        remote(ref, ref, p_s.at[q], p_r.at[q], sibling).wait_recv()
    w_pass(4)
    wf_copy().start()
    w_arrive(0, 2)
    w_pass(2)
    x_forward(1, (2, 3))
    for d in (1, 3, 2):
        w_arrive(1, d)
        wc_copy(2, d).start()
    for d in (1, 3, 2):
        o_copy(0, d).start()
    x_forward(2)
    for d in (1, 3, 2):
        o_copy(1, d).start()

    for k in range(1, NZ):
        ssz_copy(k).wait_recv()
    total = ssz[0]
    for k in range(1, NZ):
        total = total + ssz[k]
    scale = lax.rsqrt(total * (1.0 / FEATURES) + EPS)
    for b in range(4):
        rcol[b] = jnp.broadcast_to(scale[b : b + 1, :], (BLK, BLK)).T

    def normalise(shard):
        row = (shard * NX + x) * 2
        g = jnp.concatenate([gain[pl.ds(row, 1), :], gain[pl.ds(row + 1, 1), :]], axis=1)

        def one(b, carry):
            at = pl.ds(pl.multiple_of(b * BLK, BLK), BLK)
            r = rcol[b]
            v = xg[shard, at, :].astype(F32) * jnp.concatenate([r, r], axis=1) * g
            xn[at, pl.ds(pl.multiple_of(shard * 256, 256), 256)] = v.astype(BF16)
            return carry

        lax.fori_loop(0, 4, one, 0)

    normalise(z)
    normalise((z + 1) % NZ)
    normalise((z + 7) % NZ)
    normalise((z + 2) % NZ)
    normalise((z + 6) % NZ)
    def wy_pass(d):
        for e in (1, 3):
            wy_arrival(e, d).wait_recv()
            wc_copy(e, d).start()

    for d in (1, 3, 4):
        wy_pass(d)
    wf_arrival().wait_recv()
    wc_copy(2, 4).start()
    normalise((z + 3) % NZ)
    normalise((z + 5) % NZ)
    x_forward(3)
    normalise((z + 4) % NZ)
    for e in range(4):
        wc_arrival(e, 4).wait_recv()

    acc = nt_dot(xn[:, :256], wb[4, 0])
    for k in range(1, NZ):
        acc = acc + nt_dot(xn[:, k * 256 : (k + 1) * 256], wb[4, k])
    kvown[...] = acc.reshape(4, BLK, 256)
    kvs[...] = acc.astype(BF16).reshape(4, BLK, 256)

    def kv_copy(d):
        return remote(kvs.at[(x + d) % NX], kvr.at[3 - d], kv_s.at[d - 1], kv_r.at[3 - d], at_x(d))

    for d in (1, 3, 2):
        kv_copy(d).start()

    wy_pass(2)
    o_arrive(0)
    oy_copy(1).start()
    oy_copy(3).start()
    oc_copy(0).start()

    block = s * NX + x
    for d in (1, 3, 2):
        kv_copy(d).wait_recv()
    mine = kvown[x] + kvr[0].astype(F32) + kvr[1].astype(F32) + kvr[2].astype(F32)
    kvtab[block] = mine.astype(BF16)

    def ka_copy(d):
        return remote(kvtab.at[block], kvtab.at[block], ka_s.at[d - 1], ka_r.at[3 - d], at_x(d))

    def ka_arrival(d):
        ref = kvtab.at[s * NX + (x + d) % NX]
        return remote(ref, ref, ka_s.at[d - 1], ka_r.at[d - 1], at_x(d))

    def ky_copy(e, d):
        ref = kvtab.at[s * NX + (x + d) % NX]
        return remote(ref, ref, ky_s.at[e // 2, d], ky_r.at[(3 - e) // 2, d], at_y(e))

    def ky_arrival(e, d):
        ref = kvtab.at[lane_strip(e) * NX + (x + d) % NX]
        return remote(ref, ref, ky_s.at[e // 2, d], ky_r.at[e // 2, d], at_y(e))

    def kf_half(strip, d, i):
        return kvtab.at[strip * NX + (x + d) % NX, pl.ds((1 - i) * 64, 64)]

    def kf_copy(e, d):
        ref = kf_half(lane_strip(e), d, e // 2)
        return remote(ref, ref, kf_s.at[e // 2, d], kf_r.at[e // 2, d], at_y(4 - e))

    def kf_arrival(i, d):
        ref = kf_half(lane_strip(2), d, i)
        return remote(ref, ref, kf_s.at[i, d], kf_r.at[i, d], at_y(1))

    def kc_copy(e, d):
        ref = kvtab.at[lane_strip(e) * NX + (x + d) % NX]
        return remote(ref, ref, kc_s.at[e, d], kc_r.at[e, d], sibling)

    def kc_arrival(e, d):
        ref = kvtab.at[far_strip(e) * NX + (x + d) % NX]
        return remote(ref, ref, kc_s.at[e, d], kc_r.at[e, d], sibling)

    def ky_pass(d):
        for e in (1, 3):
            ky_arrival(e, d).wait_recv()
            kf_copy(e, d).start()
            kc_copy(e, d).start()

    def kf_pass(d):
        for i in range(2):
            kf_arrival(i, d).wait_recv()
        kc_copy(2, d).start()

    for d in (1, 3, 2):
        ka_copy(d).start()
    for e in (1, 3):
        ky_copy(e, 0).start()
    kc_copy(0, 0).start()

    def q_copy(xa, d):
        return remote(qs.at[xa, (x + d) % NX], qr.at[3 - d, xa], q_s.at[xa, d - 1], q_r.at[xa, 3 - d], at_x(d))

    def q_part(d, carry):
        xa = (x + d) % NX
        a = jnp.dot(xn[...], wb[d].reshape(2048, 256), preferred_element_type=F32).reshape(4, BLK, 256)
        qs[xa] = a.astype(BF16)
        qown[xa] = a
        for e in (1, 3, 2):
            q_copy(xa, e).start()
        return carry

    own_w.wait()
    for e in range(4):
        for d in range(1, 4):
            wc_arrival(e, d).wait_recv()
    lax.fori_loop(0, 4, q_part, 0)

    for d in (1, 3):
        ka_arrival(d).wait_recv()
        for e in (1, 3):
            ky_copy(e, d).start()
        kc_copy(0, d).start()
    ky_pass(0)
    ka_arrival(2).wait_recv()
    for e in (1, 3):
        ky_copy(e, 2).start()
    kc_copy(0, 2).start()
    for d in (1, 3):
        ky_pass(d)
    kf_pass(0)
    ky_pass(2)
    for d in (1, 3):
        kf_pass(d)
    o_arrive(1)
    oc_copy(2).start()
    kf_pass(2)
    for e in (1, 3):
        oy_arrival(e).wait_recv()
        oc_copy(e).start()

    for xa in range(NX):
        for d in (1, 2, 3):
            q_copy(xa, d).wait_recv()
        v = qown[xa, x] + qr[0, xa].astype(F32) + qr[1, xa].astype(F32) + qr[2, xa].astype(F32)
        qb[xa] = v.astype(BF16)

    for e in range(4):
        for d in range(4):
            kc_arrival(e, d).wait_recv()

    listed = [anc[j, block] for j in range(5)]
    tables = [kvtab[jnp.maximum(i, 0)] for i in listed] + [kvtab[block]]
    causal = lax.broadcasted_iota(jnp.int32, (BLK, BLK), 0) >= lax.broadcasted_iota(jnp.int32, (BLK, BLK), 1)
    causal = jnp.concatenate([causal, causal], axis=0)
    for xa in range(NX):
        q2 = jnp.concatenate([qb[xa, :, :HD], qb[xa, :, HD:]], axis=0)
        masks, scores = [], []
        for j in range(6):
            sc = nt_dot(q2, tables[j][:, :HD]) * HD**-0.5
            ok = causal if j == 5 else jnp.broadcast_to(listed[j], (2 * BLK, BLK)) >= 0
            masks.append(ok)
            scores.append(jnp.where(ok, sc, NEG))
        top = functools.reduce(jnp.maximum, scores)
        top = jnp.max(top, axis=1, keepdims=True)
        weights = [jnp.where(ok, jnp.exp(sc - top), 0.0) for ok, sc in zip(masks, scores)]
        total = jnp.sum(functools.reduce(jnp.add, weights), axis=1, keepdims=True)
        got = jnp.zeros((2 * BLK, HD), F32)
        for j in range(6):
            got = got + jnp.dot(weights[j].astype(BF16), tables[j][:, HD:], preferred_element_type=F32)
        got = (got / total).astype(BF16)
        attb[x, xa] = jnp.concatenate([got[:BLK], got[BLK:]], axis=1)

    def half(b, h):
        return attb.at[b, :, pl.ds(64 * h, 64)]

    def at_copy(d, h):
        return remote(half(x, h), half(x, h), at_s.at[d // 2, h], at_r.at[(3 - d) // 2, h], at_x(d))

    def at_arrival(d, h):
        ref = half((x + d) % NX, h)
        return remote(ref, ref, at_s.at[d // 2, h], at_r.at[d // 2, h], at_x(d))

    def af_copy(d):
        h = 0 if d == 1 else 1
        ref = half((x + 4 - d) % NX, h)
        return remote(ref, ref, af_s.at[h], af_r.at[h], at_x(d))

    def af_arrival(h):
        ref = half((x + 2) % NX, h)
        return remote(ref, ref, af_s.at[h], af_r.at[h], at_x(1))

    for h in range(2):
        at_copy(1, h).start()
        at_copy(3, 1 - h).start()
    for cp in own_wo:
        cp.wait()
    for e in range(4):
        oc_arrival(e).wait_recv()

    def at_ready(d, h):
        if d in (1, 3):
            at_arrival(d, h).wait_recv()
            if (d, h) in ((3, 0), (1, 1)):
                af_copy(4 - d).start()
        elif d == 2:
            af_arrival(h).wait_recv()

    def term(d, h, shard):
        b = (x + d) % NX
        at = slice(h * 64, h * 64 + 64)
        a = jnp.dot(attb[b, x, at], wob[0, shard], preferred_element_type=F32)
        for e in range(1, NX):
            a = a + jnp.dot(attb[b, (x + e) % NX, at], wob[e, shard], preferred_element_type=F32)
        return a

    def r_copy(way, k, d, h):
        step = 1 if way == 0 else -1
        at = pl.ds(h * 64, 64)
        sem = (way, k - 1, d, h)
        return remote(
            rsend.at[way, k - 1, d, at], rrecv.at[way, k - 1, d, at], rs_s.at[sem], rs_r.at[sem], at_z(step)
        )

    long_way = {0: 0, 1: 1, 3: 0, 2: 1}
    schedule = (
        (0, 0, 0, 4), (0, 1, 0, 4), (0, 0, 1, 3), (0, 1, 1, 3), (0, 0, 0, 3), (0, 0, 1, 2), (0, 1, 0, 3),
        (0, 1, 1, 2), (3, 0, 0, 4), (1, 1, 1, 4), (3, 0, 1, 3), (1, 1, 0, 3), (0, 0, 0, 2), (0, 0, 1, 1),
        (0, 1, 0, 2), (0, 1, 1, 1), (3, 1, 0, 4), (1, 0, 1, 4), (3, 1, 1, 3), (1, 0, 0, 3), (3, 0, 0, 3),
        (1, 1, 1, 3), (1, 1, 0, 2), (3, 0, 1, 2), (0, 0, 0, 1), (0, 1, 0, 1), (2, 0, 1, 4), (2, 1, 1, 4),
        (2, 0, 0, 3), (2, 1, 0, 3), (3, 1, 0, 3), (1, 0, 1, 3), (1, 0, 0, 2), (3, 1, 1, 2), (3, 0, 0, 2),
        (1, 1, 1, 2), (1, 1, 0, 1), (3, 0, 1, 1), (0, 0, -1, 0), (2, 0, 1, 3), (0, 1, -1, 0), (2, 1, 1, 3),
        (2, 0, 0, 2), (1, 0, 1, 2), (2, 1, 0, 2), (3, 1, 1, 1), (3, 1, 0, 2), (1, 1, 1, 1), (1, 0, 0, 1),
        (3, 0, 0, 1), (2, 0, 1, 2), (2, 1, 1, 2), (2, 0, 0, 1), (1, 0, 1, 1), (2, 1, 0, 1), (3, 1, 0, 1),
        (1, 1, -1, 0), (2, 0, 1, 1), (3, 0, -1, 0), (2, 1, 1, 1), (1, 0, -1, 0), (3, 1, -1, 0), (2, 0, -1, 0),
        (2, 1, -1, 0),
    )
    begun = set()
    for d, h, way, k in schedule:
        at = slice(h * 64, h * 64 + 64)
        if (d, h) not in begun:
            begun.add((d, h))
            at_ready(d, h)
        v = term(d, h, (z + (1 if way == 0 else -1) * k + NZ) % NZ)
        if k == 0:
            for one in range(2):
                r_copy(one, 1, d, h).wait_recv()
                v = v + rrecv[one, 0, d, at].astype(F32)
            out[pl.ds(pl.multiple_of(((x + d) % NX) * BLK + h * 64, 64), 64), :] = v.astype(BF16)
        else:
            if k < (4 if way == long_way[d] else 3):
                r_copy(way, k + 1, d, h).wait_recv()
                v = v + rrecv[way, k, d, at].astype(F32)
            rsend[way, k - 1, d, at] = v.astype(BF16)
            r_copy(way, k, d, h).start()

    for d, h, way, k in schedule:
        if k > 0:
            r_copy(way, k, d, h).wait_send()
    for b in range(4):
        for way in range(2):
            for hop in range(4):
                if x_used(way, hop, b):
                    x_copy(way, hop, b).wait_send()
    for i in range(2):
        for d in (1, 2, 3):
            w_copy(i, d).wait_send()
            o_copy(i, d).wait_send()
    for x2 in range(NX):
        cp = p_copy(x2)[0]

        @pl.when(jnp.logical_not(p_self(x2)))
        def _():
            cp.wait_send()

    for d in (1, 2, 3):
        ssx_copy(d).wait_send()
        kv_copy(d).wait_send()
        ka_copy(d).wait_send()
        for xa in range(NX):
            q_copy(xa, d).wait_send()
    for d in (1, 3):
        af_copy(d).wait_send()
        for h in range(2):
            at_copy(d, h).wait_send()
    for k in range(1, NZ):
        ssz_copy(k).wait_send()
    wf_copy().wait_send()
    for e in (1, 3):
        for d in range(4):
            ky_copy(e, d).wait_send()
            kf_copy(e, d).wait_send()
    for e in (1, 3):
        for d in range(1, 5):
            wy_copy(e, d).wait_send()
        oy_copy(e).wait_send()
    for e in range(4):
        for d in range(1, 5):
            wc_copy(e, d).wait_send()
        oc_copy(e).wait_send()
        for d in range(4):
            kc_copy(e, d).wait_send()


def local(tokens, norm_gain, query_weight, pair_weight, ancestors, out_weight):
    dma = pltpu.SemaphoreType.DMA
    any_ = pl.BlockSpec(memory_space=pl.ANY)
    vmem = pl.BlockSpec(memory_space=pltpu.VMEM)
    vm = pltpu.VMEM
    return pl.pallas_call(
        kernel,
        out_shape=jax.ShapeDtypeStruct((512, 256), BF16),
        in_specs=[pl.BlockSpec(memory_space=pltpu.SMEM), vmem, any_, any_, any_, any_],
        out_specs=vmem,
        scratch_shapes=[
            vm((8, 512, 256), BF16),
            vm((512, 2048), BF16),
            vm((4, 128, 128), F32),
            vm((4, 8, 128), F32),
            vm((8, 8, 128), F32),
            vm((5, 8, 256, 256), BF16),
            vm((4, 8, 256, 256), BF16),
            vm((4, 128, 256), BF16),
            vm((3, 128, 256), BF16),
            vm((4, 128, 256), F32),
            vm((32, 128, 256), BF16),
            vm((4, 4, 128, 256), BF16),
            vm((3, 4, 128, 256), BF16),
            vm((4, 4, 128, 256), F32),
            vm((4, 128, 256), BF16),
            vm((4, 4, 128, 256), BF16),
            vm((2, 4, 4, 128, 256), BF16),
            vm((2, 4, 4, 128, 256), BF16),
            dma((10,)),
            dma((2, 4, 4)), dma((2, 4, 4)), dma((3,)), dma((3,)), dma((7,)), dma((7,)),
            dma((2, 3)), dma((2, 3)), dma((4,)), dma((4,)), dma((2, 4)), dma((2, 4)), dma(()), dma(()), dma((4, 4)), dma((4, 4)),
            dma((2, 3)), dma((2, 3)), dma((2,)), dma((2,)), dma((4,)), dma((4,)),
            dma((3,)), dma((3,)), dma((3,)), dma((3,)), dma((2, 4)), dma((2, 4)), dma((2, 4)), dma((2, 4)), dma((4, 4)), dma((4, 4)),
            dma((4, 3)), dma((4, 3)), dma((2, 2)), dma((2, 2)), dma((2,)), dma((2,)), dma((2, 4, 4, 2)), dma((2, 4, 4, 2)),
        ],
        compiler_params=pltpu.CompilerParams(collective_id=0, has_side_effects=True, vmem_limit_bytes=60 << 20),
        cost_estimate=pl.CostEstimate(flops=6 * 10**9, bytes_accessed=10 << 20, transcendentals=10**6),
        name="tree_attention",
    )(
        ancestors.T,
        norm_gain.reshape(64, 128),
        tokens,
        query_weight.reshape(8, 4, 256, 256),
        pair_weight.T,
        out_weight,
    )


def solution(mesh):
    return jax.shard_map(
        local,
        mesh=mesh,
        in_specs=(P("seq", "mp"), P(), P(None, "mp"), P(None, "mp"), P(), P("mp", None)),
        out_specs=P("seq", "mp"),
        check_vma=False,
    )
```

```python
import functools

import jax
import jax.numpy as jnp
from jax import lax
from jax.experimental import pallas as pl
from jax.experimental.pallas import tpu as pltpu
from jax.sharding import PartitionSpec as P

MESH = pl.DeviceIdType.MESH
HD = 128
BLK = 128
NX, NY, NZ = 4, 4, 8
FEATURES = 8192
EPS = 1e-05
NEG = -1e30
F32 = jnp.float32
BF16 = jnp.bfloat16


def nt_dot(a, b):
    return lax.dot_general(a, b, (((1,), (1,)), ((), ())), preferred_element_type=F32)


def kernel(
    anc, gain, tok, wq, pwt, wo, out,
    xg, xn, rcol, ssx, ssz, wb, wob, kvs, kvr, kvown, kvtab, qs, qr, qown, qb, attb, rsend, rrecv,
    local_sem, x_s, x_r, ssx_s, ssx_r, ssz_s, ssz_r,
    w_s, w_r, p_s, p_r, wy_s, wy_r, wf_s, wf_r, wc_s, wc_r,
    o_s, o_r, oy_s, oy_r, oc_s, oc_r,
    kv_s, kv_r, ka_s, ka_r, ky_s, ky_r, kf_s, kf_r, kc_s, kc_r, q_s, q_r, at_s, at_r, af_s, af_r, rs_s, rs_r,
):
    s = lax.axis_index("seq")
    m = lax.axis_index("mp")
    y, c = s // 2, s % 2
    z, x = m // NX, m % NX

    def at_x(d):
        return (s, z * NX + (x + d) % NX)

    def at_z(k):
        return (s, ((z + k + NZ) % NZ) * NX + x)

    def at_y(e):
        return (((y + e) % NY) * 2 + c, m)

    sibling = (y * 2 + 1 - c, m)

    def lane_strip(e):
        return ((y + e) % NY) * 2 + c

    def far_strip(e):
        return ((y + e) % NY) * 2 + 1 - c

    def remote(src, dst, ss, rs, dev):
        return pltpu.make_async_remote_copy(
            src_ref=src, dst_ref=dst, send_sem=ss, recv_sem=rs, device_id=dev, device_id_type=MESH
        )

    pair_q = (m // 16) * 2 + m % 2
    pair_z = (m // 2) % NZ

    barrier = pltpu.get_barrier_semaphore()
    peers = [at_x(d) for d in (1, 2, 3)] + [at_z(k) for k in range(1, NZ)] + [at_y(e) for e in (1, 2, 3)] + [sibling]
    for dev in peers:
        pl.semaphore_signal(barrier, inc=1, device_id=dev, device_id_type=MESH)
    for source in (2 * z, 2 * z + 1, 16 + 2 * z, 17 + 2 * z):

        @pl.when(source != m)
        def _():
            pl.semaphore_signal(barrier, inc=1, device_id=(s, source), device_id_type=MESH)

    own_x = pltpu.make_async_copy(tok, xg.at[z], local_sem.at[0])
    own_x.start()
    own_w = pltpu.make_async_copy(wq.at[:, x], wb.at[0], local_sem.at[1])
    own_w.start()
    pl.semaphore_wait(barrier, len(peers) + jnp.where(pair_z == z, 3, 4))

    def rows(b):
        return pl.ds(b * BLK, BLK)

    def x_copy(way, hop, b):
        step = 1 if way == 0 else -1
        shard = (z - step * hop + NZ) % NZ
        src = tok.at[rows(b)] if hop == 0 else xg.at[shard, rows(b)]
        return remote(src, xg.at[shard, rows(b)], x_s.at[way, hop, b], x_r.at[way, hop, b], at_z(step))

    def x_arrival(way, hop, b):
        step = 1 if way == 0 else -1
        shard = (z - step * (hop + 1) + NZ) % NZ
        ref = xg.at[shard, rows(b)]
        return remote(ref, ref, x_s.at[way, hop, b], x_r.at[way, hop, b], at_z(step))

    def x_used(way, hop, b):
        return hop < 3 or (b < 2) == (way == 0)

    for b in range(2):
        for way in range(2):
            x_copy(way, 0, b).start()

    def w_copy(i, d):
        strip = lane_strip(2 * i)
        return remote(wq.at[strip, (x + d) % NX], wb.at[4 - d, strip], w_s.at[i, d - 1], w_r.at[i, 3 - d], at_x(d))

    def p_copy(x2):
        src = pwt.at[:, pl.ds(pl.multiple_of((s * NX + x2) * 256, 256), 256)]
        dst = wb.at[4, s, pl.ds(pl.multiple_of(pair_q * 64, 64), 64), :]
        return remote(src, dst, p_s.at[x2], p_r.at[pair_q], (s, pair_z * NX + x2)), src, dst

    def p_self(x2):
        return jnp.logical_and(pair_z == z, x == x2)

    for x2 in range(NX):
        cp, src, dst = p_copy(x2)

        @pl.when(p_self(x2))
        def _():
            pltpu.make_async_copy(src, dst, p_r.at[pair_q]).start()

        @pl.when(jnp.logical_not(p_self(x2)))
        def _():
            cp.start()

    for d in (1, 3, 2):
        w_copy(0, d).start()
    for b in range(2, 4):
        for way in range(2):
            x_copy(way, 0, b).start()

    own_x.wait()
    row_id = lax.broadcasted_iota(jnp.int32, (8, BLK), 0)
    part = jnp.zeros((8, BLK), F32)
    for b in range(4):
        xf = xg[z, b * BLK : (b + 1) * BLK, :].astype(F32)
        sums = jnp.broadcast_to(jnp.sum(xf * xf, axis=1, keepdims=True), (BLK, BLK)).T
        part = jnp.where(row_id == b, sums[:8], part)
    ssx[0] = part

    def ssx_copy(d):
        return remote(ssx.at[0], ssx.at[4 - d], ssx_s.at[d - 1], ssx_r.at[3 - d], at_x(d))

    def ssz_copy(k):
        return remote(ssz.at[0], ssz.at[NZ - k], ssz_s.at[k - 1], ssz_r.at[NZ - 1 - k], at_z(k))

    for d in (1, 3, 2):
        ssx_copy(d).start()

    def x_forward(hop, blocks=range(4)):
        for b in blocks:
            for way in range(2):
                if x_used(way, hop, b):
                    x_arrival(way, hop, b).wait_recv()
                    if hop < 3 and x_used(way, hop + 1, b):
                        x_copy(way, hop + 1, b).start()

    def wy_copy(e, d):
        src = wb.at[d, s]
        return remote(src, src, wy_s.at[e // 2, d - 1], wy_r.at[(3 - e) // 2, d - 1], at_y(e))

    def wy_arrival(e, d):
        ref = wb.at[d, lane_strip(e)]
        return remote(ref, ref, wy_s.at[e // 2, d - 1], wy_r.at[e // 2, d - 1], at_y(e))

    def wf_copy():
        src = wb.at[4, s]
        return remote(src, src, wf_s, wf_r, at_y(2))

    def wf_arrival():
        ref = wb.at[4, lane_strip(2)]
        return remote(ref, ref, wf_s, wf_r, at_y(2))

    def wc_copy(e, d):
        src = wb.at[d, lane_strip(e)]
        return remote(src, src, wc_s.at[e, d - 1], wc_r.at[e, d - 1], sibling)

    def wc_arrival(e, d):
        ref = wb.at[d, far_strip(e)]
        return remote(ref, ref, wc_s.at[e, d - 1], wc_r.at[e, d - 1], sibling)

    def w_arrive(i, d):
        ref = wb.at[d, lane_strip(2 * i)]
        remote(ref, ref, w_s.at[i, d - 1], w_r.at[i, d - 1], at_x(d)).wait_recv()

    def w_pass(d):
        for e in (1, 3):
            wy_copy(e, d).start()
        wc_copy(0, d).start()

    x_forward(0, (0, 1))
    for d in (1, 2, 3):
        ssx_copy(d).wait_recv()
    ssz[0] = ssx[0] + ssx[1] + ssx[2] + ssx[3]
    for k in (1, 7, 2, 6, 3, 5, 4):
        ssz_copy(k).start()
    for d in (1, 3):
        w_arrive(0, d)
        w_pass(d)
    for d in (1, 3, 2):
        w_copy(1, d).start()
    x_forward(0, (2, 3))

    def wo_block(strip, x2):
        return wo.at[:, pl.ds(pl.multiple_of((strip * NX + x2) * 256, 256), 256)]

    own_wo = [pltpu.make_async_copy(wo_block(k, x), wob.at[0, k], local_sem.at[2 + k]) for k in range(NZ)]
    for cp in own_wo:
        cp.start()

    def o_copy(i, d):
        strip = lane_strip(2 * i)
        return remote(wo_block(strip, (x + d) % NX), wob.at[4 - d, strip], o_s.at[i, d - 1], o_r.at[i, 3 - d], at_x(d))

    def oy_copy(e):
        src = wob.at[pl.ds(1, 3), s]
        return remote(src, src, oy_s.at[e // 2], oy_r.at[(3 - e) // 2], at_y(e))

    def oy_arrival(e):
        ref = wob.at[pl.ds(1, 3), lane_strip(e)]
        return remote(ref, ref, oy_s.at[e // 2], oy_r.at[e // 2], at_y(e))

    def oc_copy(e):
        src = wob.at[pl.ds(1, 3), lane_strip(e)]
        return remote(src, src, oc_s.at[e], oc_r.at[e], sibling)

    def oc_arrival(e):
        ref = wob.at[pl.ds(1, 3), far_strip(e)]
        return remote(ref, ref, oc_s.at[e], oc_r.at[e], sibling)

    def o_arrive(i):
        strip = lane_strip(2 * i)
        for d in (1, 2, 3):
            ref = wob.at[d, strip]
            remote(ref, ref, o_s.at[i, d - 1], o_r.at[i, d - 1], at_x(d)).wait_recv()

    x_forward(1, (0, 1))
    for q in range(4):
        ref = wb.at[4, s, pl.ds(q * 64, 64), :]
        remote(ref, ref, p_s.at[q], p_r.at[q], sibling).wait_recv()
    w_pass(4)
    wf_copy().start()
    w_arrive(0, 2)
    w_pass(2)
    x_forward(1, (2, 3))
    for d in (1, 3, 2):
        w_arrive(1, d)
        wc_copy(2, d).start()
    for d in (1, 3, 2):
        o_copy(0, d).start()
    x_forward(2)
    for d in (1, 3, 2):
        o_copy(1, d).start()

    for k in range(1, NZ):
        ssz_copy(k).wait_recv()
    total = ssz[0]
    for k in range(1, NZ):
        total = total + ssz[k]
    scale = lax.rsqrt(total * (1.0 / FEATURES) + EPS)
    for b in range(4):
        rcol[b] = jnp.broadcast_to(scale[b : b + 1, :], (BLK, BLK)).T

    def normalise(shard):
        row = (shard * NX + x) * 2
        g = jnp.concatenate([gain[pl.ds(row, 1), :], gain[pl.ds(row + 1, 1), :]], axis=1)

        def one(b, carry):
            at = pl.ds(pl.multiple_of(b * BLK, BLK), BLK)
            r = rcol[b]
            v = xg[shard, at, :].astype(F32) * jnp.concatenate([r, r], axis=1) * g
            xn[at, pl.ds(pl.multiple_of(shard * 256, 256), 256)] = v.astype(BF16)
            return carry

        lax.fori_loop(0, 4, one, 0)

    normalise(z)
    normalise((z + 1) % NZ)
    normalise((z + 7) % NZ)
    normalise((z + 2) % NZ)
    normalise((z + 6) % NZ)
    def wy_pass(d):
        for e in (1, 3):
            wy_arrival(e, d).wait_recv()
            wc_copy(e, d).start()

    for d in (1, 3, 4):
        wy_pass(d)
    wf_arrival().wait_recv()
    wc_copy(2, 4).start()
    o_arrive(0)
    oy_copy(1).start()
    oy_copy(3).start()
    oc_copy(0).start()
    normalise((z + 3) % NZ)
    normalise((z + 5) % NZ)
    x_forward(3)
    normalise((z + 4) % NZ)
    for e in range(4):
        wc_arrival(e, 4).wait_recv()

    acc = nt_dot(xn[:, :256], wb[4, 0])
    for k in range(1, NZ):
        acc = acc + nt_dot(xn[:, k * 256 : (k + 1) * 256], wb[4, k])
    kvown[...] = acc.reshape(4, BLK, 256)
    kvs[...] = acc.astype(BF16).reshape(4, BLK, 256)

    def kv_copy(d):
        return remote(kvs.at[(x + d) % NX], kvr.at[3 - d], kv_s.at[d - 1], kv_r.at[3 - d], at_x(d))

    for d in (1, 3, 2):
        kv_copy(d).start()

    wy_pass(2)

    block = s * NX + x
    for d in (1, 3, 2):
        kv_copy(d).wait_recv()
    mine = kvown[x] + kvr[0].astype(F32) + kvr[1].astype(F32) + kvr[2].astype(F32)
    kvtab[block] = mine.astype(BF16)

    def ka_copy(d):
        return remote(kvtab.at[block], kvtab.at[block], ka_s.at[d - 1], ka_r.at[3 - d], at_x(d))

    def ka_arrival(d):
        ref = kvtab.at[s * NX + (x + d) % NX]
        return remote(ref, ref, ka_s.at[d - 1], ka_r.at[d - 1], at_x(d))

    def ky_copy(e, d):
        ref = kvtab.at[s * NX + (x + d) % NX]
        return remote(ref, ref, ky_s.at[e // 2, d], ky_r.at[(3 - e) // 2, d], at_y(e))

    def ky_arrival(e, d):
        ref = kvtab.at[lane_strip(e) * NX + (x + d) % NX]
        return remote(ref, ref, ky_s.at[e // 2, d], ky_r.at[e // 2, d], at_y(e))

    def kf_half(strip, d, i):
        return kvtab.at[strip * NX + (x + d) % NX, pl.ds((1 - i) * 64, 64)]

    def kf_copy(e, d):
        ref = kf_half(lane_strip(e), d, e // 2)
        return remote(ref, ref, kf_s.at[e // 2, d], kf_r.at[e // 2, d], at_y(4 - e))

    def kf_arrival(i, d):
        ref = kf_half(lane_strip(2), d, i)
        return remote(ref, ref, kf_s.at[i, d], kf_r.at[i, d], at_y(1))

    def kc_copy(e, d):
        ref = kvtab.at[lane_strip(e) * NX + (x + d) % NX]
        return remote(ref, ref, kc_s.at[e, d], kc_r.at[e, d], sibling)

    def kc_arrival(e, d):
        ref = kvtab.at[far_strip(e) * NX + (x + d) % NX]
        return remote(ref, ref, kc_s.at[e, d], kc_r.at[e, d], sibling)

    def ky_pass(d):
        for e in (1, 3):
            ky_arrival(e, d).wait_recv()
            kf_copy(e, d).start()
            kc_copy(e, d).start()

    def kf_pass(d):
        for i in range(2):
            kf_arrival(i, d).wait_recv()
        kc_copy(2, d).start()

    for d in (1, 3, 2):
        ka_copy(d).start()
    for e in (1, 3):
        ky_copy(e, 0).start()
    kc_copy(0, 0).start()

    def q_copy(xa, d):
        return remote(qs.at[xa, (x + d) % NX], qr.at[3 - d, xa], q_s.at[xa, d - 1], q_r.at[xa, 3 - d], at_x(d))

    def q_part(d, carry):
        xa = (x + d) % NX
        a = jnp.dot(xn[...], wb[d].reshape(2048, 256), preferred_element_type=F32).reshape(4, BLK, 256)
        qs[xa] = a.astype(BF16)
        qown[xa] = a
        for e in (1, 3, 2):
            q_copy(xa, e).start()
        return carry

    own_w.wait()
    for e in range(4):
        for d in range(1, 4):
            wc_arrival(e, d).wait_recv()
    lax.fori_loop(0, 4, q_part, 0)
    o_arrive(1)
    oc_copy(2).start()

    for d in (1, 3):
        ka_arrival(d).wait_recv()
        for e in (1, 3):
            ky_copy(e, d).start()
        kc_copy(0, d).start()
    ky_pass(0)
    ka_arrival(2).wait_recv()
    for e in (1, 3):
        ky_copy(e, 2).start()
    kc_copy(0, 2).start()
    for d in (1, 3):
        ky_pass(d)
    for e in (1, 3):
        oy_arrival(e).wait_recv()
        oc_copy(e).start()
    kf_pass(0)
    ky_pass(2)
    for d in (1, 3):
        kf_pass(d)
    kf_pass(2)

    for xa in range(NX):
        for d in (1, 2, 3):
            q_copy(xa, d).wait_recv()
        v = qown[xa, x] + qr[0, xa].astype(F32) + qr[1, xa].astype(F32) + qr[2, xa].astype(F32)
        qb[xa] = v.astype(BF16)

    for e in range(4):
        for d in range(4):
            kc_arrival(e, d).wait_recv()

    listed = [anc[j, block] for j in range(5)]
    tables = [kvtab[jnp.maximum(i, 0)] for i in listed] + [kvtab[block]]
    causal = lax.broadcasted_iota(jnp.int32, (BLK, BLK), 0) >= lax.broadcasted_iota(jnp.int32, (BLK, BLK), 1)
    causal = jnp.concatenate([causal, causal], axis=0)
    for xa in range(NX):
        q2 = jnp.concatenate([qb[xa, :, :HD], qb[xa, :, HD:]], axis=0)
        masks, scores = [], []
        for j in range(6):
            sc = nt_dot(q2, tables[j][:, :HD]) * HD**-0.5
            ok = causal if j == 5 else jnp.broadcast_to(listed[j], (2 * BLK, BLK)) >= 0
            masks.append(ok)
            scores.append(jnp.where(ok, sc, NEG))
        top = functools.reduce(jnp.maximum, scores)
        top = jnp.max(top, axis=1, keepdims=True)
        weights = [jnp.where(ok, jnp.exp(sc - top), 0.0) for ok, sc in zip(masks, scores)]
        total = jnp.sum(functools.reduce(jnp.add, weights), axis=1, keepdims=True)
        got = jnp.zeros((2 * BLK, HD), F32)
        for j in range(6):
            got = got + jnp.dot(weights[j].astype(BF16), tables[j][:, HD:], preferred_element_type=F32)
        got = (got / total).astype(BF16)
        attb[x, xa] = jnp.concatenate([got[:BLK], got[BLK:]], axis=1)

    def half(b, h):
        return attb.at[b, :, pl.ds(64 * h, 64)]

    def at_copy(d, h):
        return remote(half(x, h), half(x, h), at_s.at[d // 2, h], at_r.at[(3 - d) // 2, h], at_x(d))

    def at_arrival(d, h):
        ref = half((x + d) % NX, h)
        return remote(ref, ref, at_s.at[d // 2, h], at_r.at[d // 2, h], at_x(d))

    def af_copy(d):
        h = 0 if d == 1 else 1
        ref = half((x + 4 - d) % NX, h)
        return remote(ref, ref, af_s.at[h], af_r.at[h], at_x(d))

    def af_arrival(h):
        ref = half((x + 2) % NX, h)
        return remote(ref, ref, af_s.at[h], af_r.at[h], at_x(1))

    for h in range(2):
        at_copy(1, h).start()
        at_copy(3, 1 - h).start()
    for cp in own_wo:
        cp.wait()
    for e in range(4):
        oc_arrival(e).wait_recv()

    def at_ready(d, h):
        if d in (1, 3):
            at_arrival(d, h).wait_recv()
            if (d, h) in ((3, 0), (1, 1)):
                af_copy(4 - d).start()
        elif d == 2:
            af_arrival(h).wait_recv()

    def term(d, h, shard):
        b = (x + d) % NX
        at = slice(h * 64, h * 64 + 64)
        a = jnp.dot(attb[b, x, at], wob[0, shard], preferred_element_type=F32)
        for e in range(1, NX):
            a = a + jnp.dot(attb[b, (x + e) % NX, at], wob[e, shard], preferred_element_type=F32)
        return a

    def r_copy(way, k, d, h):
        step = 1 if way == 0 else -1
        at = pl.ds(h * 64, 64)
        sem = (way, k - 1, d, h)
        return remote(
            rsend.at[way, k - 1, d, at], rrecv.at[way, k - 1, d, at], rs_s.at[sem], rs_r.at[sem], at_z(step)
        )

    long_way = {0: 0, 1: 1, 3: 0, 2: 1}
    schedule = (
        (0, 0, 0, 4), (0, 1, 0, 4), (0, 0, 1, 3), (0, 1, 1, 3), (0, 0, 0, 3), (0, 0, 1, 2), (0, 1, 0, 3),
        (0, 1, 1, 2), (3, 0, 0, 4), (1, 1, 1, 4), (3, 0, 1, 3), (1, 1, 0, 3), (0, 0, 0, 2), (0, 0, 1, 1),
        (0, 1, 0, 2), (0, 1, 1, 1), (3, 1, 0, 4), (1, 0, 1, 4), (3, 1, 1, 3), (1, 0, 0, 3), (3, 0, 0, 3),
        (1, 1, 1, 3), (1, 1, 0, 2), (3, 0, 1, 2), (0, 0, 0, 1), (0, 1, 0, 1), (2, 0, 1, 4), (2, 1, 1, 4),
        (2, 0, 0, 3), (2, 1, 0, 3), (3, 1, 0, 3), (1, 0, 1, 3), (1, 0, 0, 2), (3, 1, 1, 2), (3, 0, 0, 2),
        (1, 1, 1, 2), (1, 1, 0, 1), (3, 0, 1, 1), (0, 0, -1, 0), (2, 0, 1, 3), (0, 1, -1, 0), (2, 1, 1, 3),
        (2, 0, 0, 2), (1, 0, 1, 2), (2, 1, 0, 2), (3, 1, 1, 1), (3, 1, 0, 2), (1, 1, 1, 1), (1, 0, 0, 1),
        (3, 0, 0, 1), (2, 0, 1, 2), (2, 1, 1, 2), (2, 0, 0, 1), (1, 0, 1, 1), (2, 1, 0, 1), (3, 1, 0, 1),
        (1, 1, -1, 0), (2, 0, 1, 1), (3, 0, -1, 0), (2, 1, 1, 1), (1, 0, -1, 0), (3, 1, -1, 0), (2, 0, -1, 0),
        (2, 1, -1, 0),
    )
    begun = set()
    for d, h, way, k in schedule:
        at = slice(h * 64, h * 64 + 64)
        if (d, h) not in begun:
            begun.add((d, h))
            at_ready(d, h)
        v = term(d, h, (z + (1 if way == 0 else -1) * k + NZ) % NZ)
        if k == 0:
            for one in range(2):
                r_copy(one, 1, d, h).wait_recv()
                v = v + rrecv[one, 0, d, at].astype(F32)
            out[pl.ds(pl.multiple_of(((x + d) % NX) * BLK + h * 64, 64), 64), :] = v.astype(BF16)
        else:
            if k < (4 if way == long_way[d] else 3):
                r_copy(way, k + 1, d, h).wait_recv()
                v = v + rrecv[way, k, d, at].astype(F32)
            rsend[way, k - 1, d, at] = v.astype(BF16)
            r_copy(way, k, d, h).start()

    for d, h, way, k in schedule:
        if k > 0:
            r_copy(way, k, d, h).wait_send()
    for b in range(4):
        for way in range(2):
            for hop in range(4):
                if x_used(way, hop, b):
                    x_copy(way, hop, b).wait_send()
    for i in range(2):
        for d in (1, 2, 3):
            w_copy(i, d).wait_send()
            o_copy(i, d).wait_send()
    for x2 in range(NX):
        cp = p_copy(x2)[0]

        @pl.when(jnp.logical_not(p_self(x2)))
        def _():
            cp.wait_send()

    for d in (1, 2, 3):
        ssx_copy(d).wait_send()
        kv_copy(d).wait_send()
        ka_copy(d).wait_send()
        for xa in range(NX):
            q_copy(xa, d).wait_send()
    for d in (1, 3):
        af_copy(d).wait_send()
        for h in range(2):
            at_copy(d, h).wait_send()
    for k in range(1, NZ):
        ssz_copy(k).wait_send()
    wf_copy().wait_send()
    for e in (1, 3):
        for d in range(4):
            ky_copy(e, d).wait_send()
            kf_copy(e, d).wait_send()
    for e in (1, 3):
        for d in range(1, 5):
            wy_copy(e, d).wait_send()
        oy_copy(e).wait_send()
    for e in range(4):
        for d in range(1, 5):
            wc_copy(e, d).wait_send()
        oc_copy(e).wait_send()
        for d in range(4):
            kc_copy(e, d).wait_send()


def local(tokens, norm_gain, query_weight, pair_weight, ancestors, out_weight):
    dma = pltpu.SemaphoreType.DMA
    any_ = pl.BlockSpec(memory_space=pl.ANY)
    vmem = pl.BlockSpec(memory_space=pltpu.VMEM)
    vm = pltpu.VMEM
    return pl.pallas_call(
        kernel,
        out_shape=jax.ShapeDtypeStruct((512, 256), BF16),
        in_specs=[pl.BlockSpec(memory_space=pltpu.SMEM), vmem, any_, any_, any_, any_],
        out_specs=vmem,
        scratch_shapes=[
            vm((8, 512, 256), BF16),
            vm((512, 2048), BF16),
            vm((4, 128, 128), F32),
            vm((4, 8, 128), F32),
            vm((8, 8, 128), F32),
            vm((5, 8, 256, 256), BF16),
            vm((4, 8, 256, 256), BF16),
            vm((4, 128, 256), BF16),
            vm((3, 128, 256), BF16),
            vm((4, 128, 256), F32),
            vm((32, 128, 256), BF16),
            vm((4, 4, 128, 256), BF16),
            vm((3, 4, 128, 256), BF16),
            vm((4, 4, 128, 256), F32),
            vm((4, 128, 256), BF16),
            vm((4, 4, 128, 256), BF16),
            vm((2, 4, 4, 128, 256), BF16),
            vm((2, 4, 4, 128, 256), BF16),
            dma((10,)),
            dma((2, 4, 4)), dma((2, 4, 4)), dma((3,)), dma((3,)), dma((7,)), dma((7,)),
            dma((2, 3)), dma((2, 3)), dma((4,)), dma((4,)), dma((2, 4)), dma((2, 4)), dma(()), dma(()), dma((4, 4)), dma((4, 4)),
            dma((2, 3)), dma((2, 3)), dma((2,)), dma((2,)), dma((4,)), dma((4,)),
            dma((3,)), dma((3,)), dma((3,)), dma((3,)), dma((2, 4)), dma((2, 4)), dma((2, 4)), dma((2, 4)), dma((4, 4)), dma((4, 4)),
            dma((4, 3)), dma((4, 3)), dma((2, 2)), dma((2, 2)), dma((2,)), dma((2,)), dma((2, 4, 4, 2)), dma((2, 4, 4, 2)),
        ],
        compiler_params=pltpu.CompilerParams(collective_id=0, has_side_effects=True, vmem_limit_bytes=60 << 20),
        cost_estimate=pl.CostEstimate(flops=6 * 10**9, bytes_accessed=10 << 20, transcendentals=10**6),
        name="tree_attention",
    )(
        ancestors.T,
        norm_gain.reshape(64, 128),
        tokens,
        query_weight.reshape(8, 4, 256, 256),
        pair_weight.T,
        out_weight,
    )


def solution(mesh):
    return jax.shard_map(
        local,
        mesh=mesh,
        in_specs=(P("seq", "mp"), P(), P(None, "mp"), P(None, "mp"), P(), P("mp", None)),
        out_specs=P("seq", "mp"),
        check_vma=False,
    )
```
